256 devices in a mesh: gx: 8 (over z), gy: 32 (over y, x, core).
Axes of the slice: x: 4, y: 4, z: 8, core: 2. Of those that a mesh axis runs over, the one named last changes fastest.
Arguments:
- tokens: bfloat16 [512, 8192], P('gy', 'gx'), may hold values from -6 to 6
- gate_projection_weight: bfloat16 [8192, 28672], P('gx', 'gy'), may hold values from -0.0625 to 0.0625
- upward_projection_weight: bfloat16 [8192, 28672], P('gx', 'gy'), may hold values from -0.0625 to 0.0625
- down_projection_weight: bfloat16 [28672, 8192], P('gy', 'gx'), may hold values from -0.03125 to 0.03125
- gate_adapter_input_map: bfloat16 [8192, 64], P('gx'), may hold values from -0.0625 to 0.0625
- up_adapter_input_map: bfloat16 [8192, 64], P('gx'), may hold values from -0.0625 to 0.0625
- down_adapter_input_map: bfloat16 [28672, 64], P('gy'), may hold values from -0.03125 to 0.03125
- gate_adapter_output_map: bfloat16 [64, 28672], P(None, 'gy'), may hold values from -0.75 to 0.75
- up_adapter_output_map: bfloat16 [64, 28672], P(None, 'gy'), may hold values from -0.75 to 0.75
- down_adapter_output_map: bfloat16 [64, 8192], P(None, 'gx'), may hold values from -0.75 to 0.75
- cotangent: bfloat16 [512, 8192], P('gy', 'gx'), may hold values from -6 to 6
Outputs:
- output: bfloat16 [512, 8192], P('gy', 'gx')
- token_input_gradient: bfloat16 [512, 8192], P('gy', 'gx')
- gate_output_map_gradient: float32 [64, 28672], P('gx', 'gy')
- up_output_map_gradient: float32 [64, 28672], P('gx', 'gy')
- down_output_map_gradient: float32 [64, 8192], P('gy', 'gx')
The draws below stay inside these ranges and needn't reach their ends.
All inputs are finite; a program needn't handle non-finite values.
Results may differ from the reference program's by a relative error of at most 0.02.
Values may be sent and summed in bfloat16 or wider, within the bound.
A program may use at most 64 MiB of HBM per device.

```python
import jax
import jax.numpy as jnp

D = 8192
FF = 28672
RANK = 64
TOKENS = 512


def shard_levels(stream_key, shape, pieces, least, largest):
    loudness = 1.0
    for axis_at, parts in pieces:
        steps = jax.random.uniform(jax.random.fold_in(jax.random.fold_in(stream_key, 6), axis_at), (parts,), jnp.float32, least / len(pieces), largest / len(pieces))
        loudness = loudness * jnp.repeat(jnp.exp(steps), shape[axis_at] // parts).reshape((-1,) + (1,) * (len(shape) - 1 - axis_at))
    return loudness


def gaussian(own_key, shape, width, reach, split=(), dtype=jnp.bfloat16):
    entries = width * jax.random.normal(own_key, shape, jnp.float32)
    if split:
        entries = entries * shard_levels(own_key, shape, split, -0.22, 0.18)
    return jnp.clip(entries, -reach, reach).astype(dtype)


def setup_inputs(seed: int = 0) -> dict:
    keys = jax.random.split(jax.random.key(seed), 12)
    return {
        "tokens": gaussian(keys[0], (TOKENS, D), 1.0, 6.0, ((0, 32), (1, 8))),
        "gate_projection_weight": gaussian(keys[1], (D, FF), D ** -0.5, 0.0625, ((0, 8), (1, 32))),
        "upward_projection_weight": gaussian(keys[2], (D, FF), D ** -0.5, 0.0625, ((0, 8), (1, 32))),
        "down_projection_weight": gaussian(keys[3], (FF, D), FF ** -0.5, 0.03125, ((0, 32), (1, 8))),
        "gate_adapter_input_map": gaussian(keys[4], (D, RANK), D ** -0.5, 0.0625, ((0, 8),)),
        "up_adapter_input_map": gaussian(keys[5], (D, RANK), D ** -0.5, 0.0625, ((0, 8),)),
        "down_adapter_input_map": gaussian(keys[6], (FF, RANK), FF ** -0.5, 0.03125, ((0, 32),)),
        "gate_adapter_output_map": gaussian(keys[7], (RANK, FF), RANK ** -0.5, 0.75, ((1, 32),)),
        "up_adapter_output_map": gaussian(keys[8], (RANK, FF), RANK ** -0.5, 0.75, ((1, 32),)),
        "down_adapter_output_map": gaussian(keys[9], (RANK, D), RANK ** -0.5, 0.75, ((1, 8),)),
        "cotangent": gaussian(keys[10], (TOKENS, D), 1.0, 6.0, ((0, 32), (1, 8))),
    }


adapter_scale = 0.5


def gated_product(left, right):
    return jnp.dot(left, right, preferred_element_type=jnp.float32)


def reference(tokens, gate_projection_weight, upward_projection_weight, down_projection_weight, gate_adapter_input_map, up_adapter_input_map, down_adapter_input_map, gate_adapter_output_map, up_adapter_output_map, down_adapter_output_map, cotangent):
    gate_reduced = gated_product(tokens, gate_adapter_input_map).astype(jnp.bfloat16)
    upward_reduced = gated_product(tokens, up_adapter_input_map).astype(jnp.bfloat16)
    gate_activation = gated_product(tokens, gate_projection_weight) + adapter_scale * gated_product(gate_reduced, gate_adapter_output_map)
    upward_activation = gated_product(tokens, upward_projection_weight) + adapter_scale * gated_product(upward_reduced, up_adapter_output_map)
    hidden_state = (jax.nn.silu(gate_activation) * upward_activation).astype(jnp.bfloat16)
    down_reduced = gated_product(hidden_state, down_adapter_input_map).astype(jnp.bfloat16)
    output = (gated_product(hidden_state, down_projection_weight) + adapter_scale * gated_product(down_reduced, down_adapter_output_map)).astype(jnp.bfloat16)
    down_output_map_gradient = adapter_scale * gated_product(down_reduced.T, cotangent)
    down_backward = gated_product(cotangent, down_adapter_output_map.T).astype(jnp.bfloat16)
    hidden_gradient = gated_product(cotangent, down_projection_weight.T) + adapter_scale * gated_product(down_backward, down_adapter_input_map.T)
    sigma = jax.nn.sigmoid(gate_activation)
    gate_gradient = (hidden_gradient * upward_activation * sigma * (1.0 + gate_activation * (1.0 - sigma))).astype(jnp.bfloat16)
    upward_gradient = (hidden_gradient * gate_activation * sigma).astype(jnp.bfloat16)
    gate_output_map_gradient = adapter_scale * gated_product(gate_reduced.T, gate_gradient)
    up_output_map_gradient = adapter_scale * gated_product(upward_reduced.T, upward_gradient)
    gate_backward = gated_product(gate_gradient, gate_adapter_output_map.T).astype(jnp.bfloat16)
    upward_backward = gated_product(upward_gradient, up_adapter_output_map.T).astype(jnp.bfloat16)
    token_input_gradient = gated_product(gate_gradient, gate_projection_weight.T) + gated_product(upward_gradient, upward_projection_weight.T)
    token_input_gradient = token_input_gradient + adapter_scale * (gated_product(gate_backward, gate_adapter_input_map.T) + gated_product(upward_backward, up_adapter_input_map.T))
    return output, token_input_gradient.astype(jnp.bfloat16), gate_output_map_gradient, up_output_map_gradient, down_output_map_gradient
```

```python
import functools

import jax
import jax.numpy as jnp
from jax import lax
from jax.experimental import pallas as pl
from jax.experimental.pallas import tpu as pltpu
from jax.sharding import PartitionSpec as P

MESH = pl.DeviceIdType.MESH
F32 = jnp.float32
BF16 = jnp.bfloat16

NZ = 8
NG = 32
SIDE = 4
NC = 16
TB = 16
CH = 64
D = 1024
FF = 896
R = 64
W = D + 128
SCALE = 0.5


def nn(left, right):
    return jnp.dot(left, right, preferred_element_type=F32)


def nt(left, right):
    return lax.dot_general(left, right, (((1,), (1,)), ((), ())), preferred_element_type=F32)


def tn(left, right):
    return lax.dot_general(left, right, (((0,), (0,)), ((), ())), preferred_element_type=F32)


def kernel(
    tok, wg, wu, wd, ag, au, ad, bg, bu, bd, cot,
    out, tig, gmap, umap, dmap,
    X, VG, VU, VD, AG, AU, AD, BGU, BD,
    LZ, LA, DL, PG, PU, PH, GA, UA, RS, RR, H, ST, SB, O2, RX, LOWF,
    wsem, xsem, xs, xr, ys, yr, lzs, lzr, las, lar, dls, dlr, rss, rsr, ags, agr, sbs, sbr, rxs, rxr,
):
    z = lax.axis_index("gx")
    g = lax.axis_index("gy")
    q, c = g // 2, g % 2
    qx, qy = q % SIDE, q // SIDE
    sibling = g + 1 - 2 * c
    right, left = (z + 1) % NZ, (z + NZ - 1) % NZ

    def slot_of(qq, cc):
        return ((qq // 2 + 4 * cc) % NZ) * 4 + 2 * cc + qq % 2

    def chip_at(k, sign):
        dx, dy = k % SIDE, k // SIDE
        return ((qy + SIDE + sign * dy) % SIDE) * SIDE + (qx + SIDE + sign * dx) % SIDE

    def remote(src, dst, ssem, rsem, zz, gg):
        return pltpu.make_async_remote_copy(
            src_ref=src, dst_ref=dst, send_sem=ssem, recv_sem=rsem, device_id=(zz, gg), device_id_type=MESH
        )

    me = slot_of(q, c)

    own_copies = [
        pltpu.make_async_copy(tok, X.at[0, me], xsem.at[0]),
        pltpu.make_async_copy(cot, X.at[1, me], xsem.at[1]),
    ]
    low_copies = [
        pltpu.make_async_copy(ag, AG, wsem.at[0]),
        pltpu.make_async_copy(au, AU, wsem.at[1]),
        pltpu.make_async_copy(bd, BD, wsem.at[2]),
    ]
    gate_copies = [
        pltpu.make_async_copy(wg, VG, wsem.at[3]),
        pltpu.make_async_copy(wu, VU, wsem.at[4]),
    ]
    rest_copies = [
        pltpu.make_async_copy(wd, VD, wsem.at[5]),
        pltpu.make_async_copy(ad, AD, wsem.at[6]),
        pltpu.make_async_copy(bg, BGU.at[pl.ds(0, R)], wsem.at[7]),
        pltpu.make_async_copy(bu, BGU.at[pl.ds(R, R)], wsem.at[8]),
    ]
    for copy in own_copies + low_copies + gate_copies + rest_copies:
        copy.start()

    barrier = pltpu.get_barrier_semaphore()

    @pl.loop(1, NG)
    def _(k):
        pl.semaphore_signal(barrier, inc=1, device_id=(z, (g + k) % NG), device_id_type=MESH)

    @pl.loop(1, NZ)
    def _(k):
        pl.semaphore_signal(barrier, inc=1, device_id=((z + k) % NZ, g), device_id_type=MESH)

    zero_half = jnp.zeros((3, CH // 2, FF), BF16)
    RR[:, 0, 3, CH // 2 : CH, :] = zero_half
    RR[:, 1, 3, 0 : CH // 2, :] = zero_half
    RR[:, :, 4] = jnp.zeros((3, 2, CH, FF), BF16)
    LZ[z] = jnp.zeros((3 * TB, 128), BF16)
    DL[me] = jnp.zeros((TB, 128), BF16)

    for copy in own_copies:
        copy.wait()
    pl.semaphore_wait(barrier, NG - 1 + NZ - 1)

    def spread_send(a):
        remote(X.at[a, me], X.at[a, me], ys.at[a, 0], yr.at[a, 0], z, sibling).start()

        @pl.loop(1, NC)
        def _(k):
            remote(X.at[a, me], X.at[a, me], xs.at[a, k], xr.at[a, k], z, 2 * chip_at(k, 1) + c).start()

    def spread_relay(a):
        @pl.loop(1, NC)
        def _(k):
            s = slot_of(chip_at(k, -1), c)
            remote(X.at[a, s], X.at[a, s], xs.at[a, k], xr.at[a, k], z, sibling).wait_recv()
            remote(X.at[a, s], X.at[a, s], ys.at[a, k], yr.at[a, k], z, sibling).start()

        @pl.loop(0, NC)
        def _(k):
            s = slot_of(chip_at(k, -1), 1 - c)
            remote(X.at[a, s], X.at[a, s], ys.at[a, k], yr.at[a, k], z, sibling).wait_recv()

    spread_send(0)

    for copy in low_copies:
        copy.wait()
    LZ[z, 0:TB, 0:R] = nn(X[0, me], AG[...]).astype(BF16)
    LZ[z, TB : 2 * TB, 0:R] = nn(X[0, me], AU[...]).astype(BF16)
    LZ[z, 2 * TB : 3 * TB, 0:R] = nt(X[1, me], BD[...]).astype(BF16)

    @pl.loop(1, NZ)
    def _(k):
        remote(LZ.at[z], LZ.at[z], lzs.at[k], lzr.at[k], (z + k) % NZ, g).start()

    spread_relay(0)
    spread_send(1)

    @pl.loop(1, NZ)
    def _(k):
        s = (z + NZ - k) % NZ
        remote(LZ.at[s], LZ.at[s], lzs.at[k], lzr.at[k], z, g).wait_recv()

    LA[me] = jnp.sum(LZ[...].astype(F32), axis=0).astype(BF16)

    @pl.loop(1, NG)
    def _(k):
        remote(LA.at[me], LA.at[me], las.at[k], lar.at[k], z, (g + k) % NG).start()

    def low_wait():
        @pl.loop(1, NG)
        def _(k):
            p = (g + NG - k) % NG
            s = slot_of(p // 2, p % 2)
            remote(LA.at[s], LA.at[s], las.at[k], lar.at[k], z, g).wait_recv()

    for copy in gate_copies + rest_copies:
        copy.wait()

    def ring_copy(a, way, j, half):
        rows = pl.ds(way * (CH // 2), CH // 2) if half else pl.ds(0, CH)
        return remote(
            RS.at[a, way, j - 1, rows], RR.at[a, way, j - 1, rows],
            rss.at[a, way, j - 1], rsr.at[a, way, j - 1], left if way else right, g,
        )

    def ring_wait(a, j):
        @pl.when(j == 3)
        def _():
            ring_copy(a, 0, 4, True).wait_recv()
            ring_copy(a, 1, 4, True).wait_recv()

        @pl.when(j < 3)
        def _():
            ring_copy(a, 0, j + 1, False).wait_recv()
            ring_copy(a, 1, j + 1, False).wait_recv()

    def pair(ref, a, j):
        da, db = (z + j) % NZ, (z + NZ - j) % NZ
        xa = ref[a, pl.ds(4 * da, 4)].reshape(CH, D)
        xb = ref[a, pl.ds(4 * db, 4)].reshape(CH, D)
        return jnp.concatenate([xa, xb], axis=0)

    def ring_step(a, part, j):
        ring_wait(a, j)

        @pl.when(j > 0)
        def _():
            RS[a, 0, j - 1] = (part[0:CH] + RR[a, 0, j].astype(F32)).astype(BF16)
            RS[a, 1, j - 1] = (part[CH : 2 * CH] + RR[a, 1, j].astype(F32)).astype(BF16)

        @pl.when(j == 4)
        def _():
            ring_copy(a, 0, 4, True).start()
            ring_copy(a, 1, 4, True).start()

        @pl.when((j > 0) & (j < 4))
        def _():
            ring_copy(a, 0, j, False).start()
            ring_copy(a, 1, j, False).start()

    def ring_total(a, part):
        return part[0:CH] + (RR[a, 0, 0].astype(F32) + RR[a, 1, 0].astype(F32))

    def low_chunk(which):
        return LA[pl.ds(4 * z, 4), which * TB : (which + 1) * TB, :].reshape(CH, 128)[:, 0:R]

    def chain_copy(b, way, j, half, arriving):
        hops = j if arriving else j - 1
        d = (z + hops) % NZ if way else (z + NZ - hops) % NZ
        rows = pl.ds(way * (CH // 2), CH // 2) if half else pl.ds(0, CH)
        return remote(
            H.at[b, d, rows], H.at[b, d, rows],
            ags.at[b, way, j - 1], agr.at[b, way, j - 1], left if way else right, g,
        )

    def chain_start(b, j):
        @pl.when(j == 4)
        def _():
            chain_copy(b, 0, 4, True, False).start()
            chain_copy(b, 1, 4, True, False).start()

        @pl.when(j < 4)
        def _():
            chain_copy(b, 0, j, False, False).start()
            chain_copy(b, 1, j, False, False).start()

    def chain_wait(b, j):
        @pl.when(j == 4)
        def _():
            chain_copy(b, 0, 4, True, True).wait_recv()
            chain_copy(b, 1, 4, True, True).wait_recv()

        @pl.when((j > 0) & (j < 4))
        def _():
            chain_copy(b, 0, j, False, True).wait_recv()
            chain_copy(b, 1, j, False, True).wait_recv()

    @pl.loop(0, 6)
    def _(i):
        @pl.when(i < 5)
        def _():
            j = 4 - i
            x = pair(X, 0, j)
            PG[...] = nn(x, VG[...])
            ring_step(0, PG, j)
            PU[...] = nn(x, VU[...])
            ring_step(1, PU, j)

            @pl.when(j == 0)
            def _():
                low_wait()
                gate = ring_total(0, PG) + SCALE * nn(low_chunk(0), BGU[0:R])
                up = ring_total(1, PU) + SCALE * nn(low_chunk(1), BGU[R : 2 * R])
                GA[...] = gate
                UA[...] = up
                H[0, z] = (gate * jax.nn.sigmoid(gate) * up).astype(BF16)
                chain_start(0, 1)

        @pl.when(i == 1)
        def _():
            spread_relay(1)

        @pl.when(i > 0)
        def _():
            j = 5 - i
            PH[...] = nt(pair(X, 1, j), VD[...])
            ring_step(2, PH, j)

            @pl.when(j == 0)
            def _():
                grad = ring_total(2, PH) + SCALE * nt(low_chunk(2), AD[...])
                gate, up = GA[...], UA[...]
                sigma = jax.nn.sigmoid(gate)
                H[1, z] = (grad * up * sigma * (1.0 + gate * (1.0 - sigma))).astype(BF16)
                H[2, z] = (grad * gate * sigma).astype(BF16)
                chain_start(1, 1)
                chain_start(2, 1)

    def sib_copy(f, d):
        rows = pl.ds(pl.multiple_of((1 - c) * 32, 32), 32)
        return remote(ST.at[f, d, rows], SB.at[f, d], sbs.at[f, d], sbr.at[f, d], z, sibling)

    def sib_start(f, j):
        da, db = (z + NZ - j) % NZ, (z + j) % NZ
        sib_copy(f, da).start()

        @pl.when((j > 0) & (j < 4))
        def _():
            sib_copy(f, db).start()

    def owner_chip(d, k):
        return 2 * ((d + 4 * c) % NZ) + k

    def owner_copy(f, d, k):
        return remote(
            O2.at[f, d, pl.ds(k * TB, TB)], RX.at[f, q], rxs.at[f, 2 * d + k], rxr.at[f, q],
            z, 2 * owner_chip(d, k) + c,
        )

    def combine_one(f, d):
        sib_copy(f, d).wait_recv()
        rows = pl.ds(pl.multiple_of(c * 32, 32), 32)
        total = (ST[f, d, rows].astype(F32) + SB[f, d].astype(F32)).astype(BF16)
        O2[f, d] = total
        for k in range(2):
            own = owner_chip(d, k) == q

            @pl.when(own)
            def _():
                RX[f, q] = total[k * TB : (k + 1) * TB]

            @pl.when(jnp.logical_not(own))
            def _():
                owner_copy(f, d, k).start()

    def combine(f, j):
        combine_one(f, (z + NZ - j) % NZ)

        @pl.when((j > 0) & (j < 4))
        def _():
            combine_one(f, (z + j) % NZ)

    def hpair(b, j):
        return jnp.concatenate([H[b, (z + NZ - j) % NZ], H[b, (z + j) % NZ]], axis=0)

    def stage(f, j, wide, low, width):
        for n, d in enumerate(((z + NZ - j) % NZ, (z + j) % NZ)):
            ST[f, d, :, 0:D] = wide[n * CH : (n + 1) * CH].astype(BF16)
            ST[f, d, :, D : D + width] = low[n * CH : (n + 1) * CH].astype(BF16)

    ST[0, :, :, D + R : W] = jnp.zeros((NZ, CH, R), BF16)

    @pl.loop(0, 5)
    def _(j):
        chain_wait(0, j)

        @pl.when((j > 0) & (j < 4))
        def _():
            chain_start(0, j + 1)

        x = hpair(0, j)
        stage(0, j, nn(x, VD[...]), nn(x, AD[...]), R)
        sib_start(0, j)

        @pl.when(j > 0)
        def _():
            combine(1, j - 1)

        chain_wait(1, j)

        @pl.when((j > 0) & (j < 4))
        def _():
            chain_start(1, j + 1)

        chain_wait(2, j)

        @pl.when((j > 0) & (j < 4))
        def _():
            chain_start(2, j + 1)

        xg, xu = hpair(1, j), hpair(2, j)
        low = jnp.where(
            lax.broadcasted_iota(jnp.int32, (2 * CH, 128), 1) < R, nt(xg, BGU[...]), nt(xu, BGU[...])
        )
        stage(1, j, nt(xg, VG[...]) + nt(xu, VU[...]), low, 128)
        sib_start(1, j)
        combine(0, j)

    combine(1, 4)

    def rows_total(f):
        @pl.loop(0, NC)
        def _(s):
            @pl.when(s != q)
            def _():
                remote(RX.at[f, s], RX.at[f, s], rxs.at[f, 0], rxr.at[f, s], z, g).wait_recv()

        return jnp.sum(RX[f].astype(F32), axis=0)

    total = rows_total(0)
    down_low = total[:, D : D + R].astype(BF16)
    DL[me, :, 0:R] = down_low

    @pl.loop(1, NG)
    def _(k):
        remote(DL.at[me], DL.at[me], dls.at[k], dlr.at[k], z, (g + k) % NG).start()

    out[...] = (total[:, 0:D] + SCALE * nn(down_low, BD[...])).astype(BF16)

    for b, ref in ((1, gmap), (2, umap)):
        low = LA[:, (b - 1) * TB : b * TB, :].reshape(NG * TB, 128)
        LOWF[...] = SCALE * tn(low, H[b].reshape(NG * TB, FF))
        ref[...] = LOWF[pl.ds(pl.multiple_of(8 * z, 8), 8)]

    total = rows_total(1)
    back = total[:, D:W].astype(BF16)
    tig[...] = (
        total[:, 0:D] + SCALE * (nt(back[:, 0:R], AG[...]) + nt(pltpu.roll(back.astype(F32), R, 1).astype(BF16)[:, 0:R], AU[...]))
    ).astype(BF16)

    @pl.loop(1, NG)
    def _(k):
        p = (g + NG - k) % NG
        s = slot_of(p // 2, p % 2)
        remote(DL.at[s], DL.at[s], dls.at[k], dlr.at[k], z, g).wait_recv()

    grads = SCALE * tn(DL[...].reshape(NG * TB, 128), X[1].reshape(NG * TB, D))
    rank = lax.broadcasted_iota(jnp.int32, (128, D), 0)
    for k in range(2):
        dmap[k : k + 1] = jnp.sum(jnp.where(rank == 2 * g + k, grads, 0.0), axis=0, keepdims=True)

    @pl.loop(1, NC)
    def _(k):
        for a in range(2):
            remote(X.at[a, me], X.at[a, me], xs.at[a, k], xr.at[a, k], z, g).wait_send()

    @pl.loop(0, NC)
    def _(k):
        for a in range(2):
            remote(X.at[a, me], X.at[a, me], ys.at[a, k], yr.at[a, k], z, g).wait_send()

    @pl.loop(1, NZ)
    def _(k):
        remote(LZ.at[z], LZ.at[z], lzs.at[k], lzr.at[k], z, g).wait_send()

    @pl.loop(1, NG)
    def _(k):
        remote(LA.at[me], LA.at[me], las.at[k], lar.at[k], z, g).wait_send()
        remote(DL.at[me], DL.at[me], dls.at[k], dlr.at[k], z, g).wait_send()

    for a in range(3):
        for way in range(2):
            ring_copy(a, way, 4, True).wait_send()
            chain_copy(a, way, 4, True, False).wait_send()

            @pl.loop(1, 4)
            def _(j):
                ring_copy(a, way, j, False).wait_send()
                chain_copy(a, way, j, False, False).wait_send()

    @pl.loop(0, NZ)
    def _(d):
        for f in range(2):
            sib_copy(f, d).wait_send()
            for k in range(2):
                @pl.when(owner_chip(d, k) != q)
                def _():
                    owner_copy(f, d, k).wait_send()


def body(*args):
    dma = pltpu.SemaphoreType.DMA
    hbm = pl.BlockSpec(memory_space=pl.ANY)
    vmem = pl.BlockSpec(memory_space=pltpu.VMEM)
    return pl.pallas_call(
        kernel,
        out_shape=(
            jax.ShapeDtypeStruct((TB, D), BF16),
            jax.ShapeDtypeStruct((TB, D), BF16),
            jax.ShapeDtypeStruct((8, FF), F32),
            jax.ShapeDtypeStruct((8, FF), F32),
            jax.ShapeDtypeStruct((2, D), F32),
        ),
        in_specs=[hbm] * 11,
        out_specs=(vmem,) * 5,
        scratch_shapes=[
            pltpu.VMEM((2, NG, TB, D), BF16),
            pltpu.VMEM((D, FF), BF16),
            pltpu.VMEM((D, FF), BF16),
            pltpu.VMEM((FF, D), BF16),
            pltpu.VMEM((D, R), BF16),
            pltpu.VMEM((D, R), BF16),
            pltpu.VMEM((FF, R), BF16),
            pltpu.VMEM((2 * R, FF), BF16),
            pltpu.VMEM((R, D), BF16),
            pltpu.VMEM((NZ, 3 * TB, 128), BF16),
            pltpu.VMEM((NG, 3 * TB, 128), BF16),
            pltpu.VMEM((NG, TB, 128), BF16),
            pltpu.VMEM((2 * CH, FF), F32),
            pltpu.VMEM((2 * CH, FF), F32),
            pltpu.VMEM((2 * CH, FF), F32),
            pltpu.VMEM((CH, FF), F32),
            pltpu.VMEM((CH, FF), F32),
            pltpu.VMEM((3, 2, 4, CH, FF), BF16),
            pltpu.VMEM((3, 2, 5, CH, FF), BF16),
            pltpu.VMEM((3, NZ, CH, FF), BF16),
            pltpu.VMEM((2, NZ, CH, W), BF16),
            pltpu.VMEM((2, NZ, CH // 2, W), BF16),
            pltpu.VMEM((2, NZ, CH // 2, W), BF16),
            pltpu.VMEM((2, NC, TB, W), BF16),
            pltpu.VMEM((128, FF), F32),
            dma((9,)),
            dma((2,)),
            dma((2, NC)),
            dma((2, NC)),
            dma((2, NC)),
            dma((2, NC)),
            dma((NZ,)),
            dma((NZ,)),
            dma((NG,)),
            dma((NG,)),
            dma((NG,)),
            dma((NG,)),
            dma((3, 2, 4)),
            dma((3, 2, 4)),
            dma((3, 2, 4)),
            dma((3, 2, 4)),
            dma((2, NZ)),
            dma((2, NZ)),
            dma((2, 2 * NZ)),
            dma((2, NC)),
        ],
        compiler_params=pltpu.CompilerParams(
            collective_id=0, has_side_effects=True, vmem_limit_bytes=48 * 1024 * 1024
        ),
    )(*args)


def solution(mesh):
    in_specs = (
        P("gy", "gx"),
        P("gx", "gy"),
        P("gx", "gy"),
        P("gy", "gx"),
        P("gx", None),
        P("gx", None),
        P("gy", None),
        P(None, "gy"),
        P(None, "gy"),
        P(None, "gx"),
        P("gy", "gx"),
    )
    out_specs = (P("gy", "gx"), P("gy", "gx"), P("gx", "gy"), P("gx", "gy"), P("gy", "gx"))
    return jax.shard_map(body, mesh=mesh, in_specs=in_specs, out_specs=out_specs, check_vma=False)
```

```python
import functools

import jax
import jax.numpy as jnp
from jax import lax
from jax.experimental import pallas as pl
from jax.experimental.pallas import tpu as pltpu
from jax.sharding import PartitionSpec as P

MESH = pl.DeviceIdType.MESH
F32 = jnp.float32
BF16 = jnp.bfloat16

NZ = 8
NG = 32
SIDE = 4
NC = 16
TB = 16
CH = 64
D = 1024
FF = 896
R = 64
W = D + 128
SCALE = 0.5
VMEM = 60 * 1024 * 1024


def mod(a, m):
    return lax.rem(a, m)


def nn(left, right):
    return jnp.dot(left, right, preferred_element_type=F32)


def nt(left, right):
    return lax.dot_general(left, right, (((1,), (1,)), ((), ())), preferred_element_type=F32)


def tn(left, right):
    return lax.dot_general(left, right, (((0,), (0,)), ((), ())), preferred_element_type=F32)


def kernel(
    tok, wg, wu, wd, ag, au, ad, bg, bu, bd, cot,
    out, tig, gmap, umap, dmap,
    X, VG, VU, VD, AGU, AD, BGU, BD,
    LZ, LA, DL, PG, PU, PH, WIDE, GA, UA, RS, RR, H, ST, SB, O2, RX, LOWF,
    wsem, xsem, xs, xr, vs, vr, ys, yr, lzs, lzr, las, lar, dls, dlr, rss, rsr, ags, agr, sbs, sbr, rxs, rxr,
):
    z = lax.axis_index("gx")
    g = lax.axis_index("gy")
    q, c = lax.div(g, 2), mod(g, 2)
    qx, qy = mod(q, SIDE), lax.div(q, SIDE)
    sibling = g + 1 - 2 * c
    right, left = mod(z + 1, NZ), mod(z + NZ - 1, NZ)

    columns = [2 * mod(qx + i, SIDE) for i in range(SIDE)]
    rows = [8 * mod(qy + i, SIDE) for i in range(SIDE)]
    first = [a + c * (b - a) for a, b in zip(columns, rows)]
    second = [b + c * (a - b) for a, b in zip(columns, rows)]

    def device_at(i, k):
        return first[i % SIDE] + second[k % SIDE] + c

    def sibling_at(i, k):
        return second[i % SIDE] + first[k % SIDE] + 1 - c

    def owner(d, cc, k):
        return 4 * mod(d + 4 * cc, NZ) + 2 * k + cc

    def owners(d):
        return [owner(d, p // 2, p % 2) for p in range(4)]

    def remote(src, dst, ssem, rsem, zz, gg):
        return pltpu.make_async_remote_copy(
            src_ref=src, dst_ref=dst, send_sem=ssem, recv_sem=rsem, device_id=(zz, gg), device_id_type=MESH
        )

    me = g

    own_copies = [
        pltpu.make_async_copy(tok, X.at[0, me], xsem.at[0]),
        pltpu.make_async_copy(cot, X.at[1, me], xsem.at[1]),
    ]
    low_copies = [
        pltpu.make_async_copy(ag, AGU.at[pl.ds(0, R)], wsem.at[0]),
        pltpu.make_async_copy(au, AGU.at[pl.ds(R, R)], wsem.at[1]),
        pltpu.make_async_copy(bd, BD, wsem.at[2]),
    ]
    gate_copies = [
        pltpu.make_async_copy(wg, VG, wsem.at[3]),
        pltpu.make_async_copy(wu, VU, wsem.at[4]),
    ]
    rest_copies = [
        pltpu.make_async_copy(wd, VD, wsem.at[5]),
        pltpu.make_async_copy(ad, AD, wsem.at[6]),
        pltpu.make_async_copy(bg, BGU.at[pl.ds(0, R)], wsem.at[7]),
        pltpu.make_async_copy(bu, BGU.at[pl.ds(R, R)], wsem.at[8]),
    ]
    for copy in own_copies + low_copies + gate_copies + rest_copies:
        copy.start()

    barrier = pltpu.get_barrier_semaphore()

    @pl.loop(1, NG)
    def _(k):
        pl.semaphore_signal(barrier, inc=1, device_id=(z, mod(g + k, NG)), device_id_type=MESH)

    @pl.loop(1, NZ)
    def _(k):
        pl.semaphore_signal(barrier, inc=1, device_id=(mod(z + k, NZ), g), device_id_type=MESH)

    zero_half = jnp.zeros((3, CH // 2, FF), BF16)
    RR[:, 0, 3, CH // 2 : CH, :] = zero_half
    RR[:, 1, 3, 0 : CH // 2, :] = zero_half
    RR[:, :, 4] = jnp.zeros((3, 2, CH, FF), BF16)
    LZ[z] = jnp.zeros((2 * TB, 128), BF16)
    DL[me] = jnp.zeros((TB, 128), BF16)

    for copy in own_copies:
        copy.wait()

    for copy in low_copies:
        copy.wait()
    LZ[z, 0:TB] = nt(X[0, me], AGU[...]).astype(BF16)
    LZ[z, TB : 2 * TB, 0:R] = nt(X[1, me], BD[...]).astype(BF16)


    pl.semaphore_wait(barrier, NG - 1 + NZ - 1)

    def near(a, s, i):
        return remote(X.at[a, s], X.at[a, s], xs.at[a, i], xr.at[a, i], z, device_at(i, 0))

    def far(a, s, i, k):
        return remote(X.at[a, s], X.at[a, s], vs.at[a, i, k], vr.at[a, i, k], z, device_at(0, k))

    def relay(a, s, i, k):
        return remote(X.at[a, s], X.at[a, s], ys.at[a, i, k], yr.at[a, i, k], z, sibling)

    def spread_near(a):
        for i in (1, 3, 2):
            near(a, me, i).start()
        relay(a, me, 0, 0).start()

    def spread_turn(a):
        for k in (1, 3, 2):
            far(a, me, 0, k).start()
        for i in (1, 3, 2):
            s = device_at(-i, 0)
            near(a, s, i).wait_recv()
            for k in (1, 3, 2):
                far(a, s, i, k).start()
            relay(a, s, i, 0).start()

    def spread_far(a):
        for k in (3, 1, 2):
            for i in (0, 1, 3, 2):
                s = device_at(-i, -k)
                far(a, s, i, k).wait_recv()
                relay(a, s, i, k).start()

    def spread_wait(a):
        for k in (0, 3, 1, 2):
            for i in (0, 1, 3, 2):
                relay(a, sibling_at(-i, -k), i, k).wait_recv()

    spread_near(0)
    spread_near(1)
    @pl.loop(1, NZ)
    def _(k):
        remote(LZ.at[z], LZ.at[z], lzs.at[k], lzr.at[k], mod(z + k, NZ), g).start()

    spread_turn(0)
    spread_turn(1)
    spread_far(0)
    spread_wait(0)

    def to_plane(ref, ssem, rsem, k):
        return remote(ref.at[me], ref.at[me], ssem.at[k], rsem.at[k], z, mod(g + k, NG))

    def from_plane(ref, ssem, rsem, k):
        s = mod(g + NG - k, NG)
        return remote(ref.at[s], ref.at[s], ssem.at[k], rsem.at[k], z, g)

    def low_sum():
        @pl.loop(1, NZ)
        def _(k):
            s = mod(z + NZ - k, NZ)
            remote(LZ.at[s], LZ.at[s], lzs.at[k], lzr.at[k], z, g).wait_recv()

        LA[me] = jnp.sum(LZ[...].astype(F32), axis=0).astype(BF16)

        @pl.loop(1, NG)
        def _(k):
            to_plane(LA, las, lar, k).start()

    def low_wait():
        @pl.loop(1, NG)
        def _(k):
            from_plane(LA, las, lar, k).wait_recv()

    for copy in gate_copies + rest_copies:
        copy.wait()

    def ring_copy(a, way, j, half):
        rows = pl.ds(way * (CH // 2), CH // 2) if half else pl.ds(0, CH)
        return remote(
            RS.at[a, way, j - 1, rows], RR.at[a, way, j - 1, rows],
            rss.at[a, way, j - 1], rsr.at[a, way, j - 1], left if way else right, g,
        )

    def ring_wait(a, j):
        @pl.when(j == 3)
        def _():
            ring_copy(a, 0, 4, True).wait_recv()
            ring_copy(a, 1, 4, True).wait_recv()

        @pl.when(j < 3)
        def _():
            ring_copy(a, 0, j + 1, False).wait_recv()
            ring_copy(a, 1, j + 1, False).wait_recv()

    def pair(a, j):
        return jnp.concatenate([X[a, p] for d in (mod(z + j, NZ), mod(z + NZ - j, NZ)) for p in owners(d)], axis=0)

    def ring_step(a, part, j):
        ring_wait(a, j)

        @pl.when(j > 0)
        def _():
            RS[a, 0, j - 1] = (part[0:CH] + RR[a, 0, j].astype(F32)).astype(BF16)
            RS[a, 1, j - 1] = (part[CH : 2 * CH] + RR[a, 1, j].astype(F32)).astype(BF16)

        @pl.when(j == 4)
        def _():
            ring_copy(a, 0, 4, True).start()
            ring_copy(a, 1, 4, True).start()

        @pl.when((j > 0) & (j < 4))
        def _():
            ring_copy(a, 0, j, False).start()
            ring_copy(a, 1, j, False).start()

    def ring_total(a, part):
        return part[0:CH] + (RR[a, 0, 0].astype(F32) + RR[a, 1, 0].astype(F32))

    def low_chunk(which):
        return jnp.concatenate([LA[p, which * TB : (which + 1) * TB] for p in owners(z)], axis=0)

    def half_rows(low, first):
        lane = lax.broadcasted_iota(jnp.int32, low.shape, 1)
        return jnp.where((lane < R) == first, low, jnp.zeros_like(low))

    def chain_copy(b, way, j, half, arriving):
        hops = j if arriving else j - 1
        d = mod(z + hops, NZ) if way else mod(z + NZ - hops, NZ)
        rows = pl.ds(way * (CH // 2), CH // 2) if half else pl.ds(0, CH)
        return remote(
            H.at[b, d, rows], H.at[b, d, rows],
            ags.at[b, way, j - 1], agr.at[b, way, j - 1], left if way else right, g,
        )

    def chain_start(b, j):
        @pl.when(j == 4)
        def _():
            chain_copy(b, 0, 4, True, False).start()
            chain_copy(b, 1, 4, True, False).start()

        @pl.when(j < 4)
        def _():
            chain_copy(b, 0, j, False, False).start()
            chain_copy(b, 1, j, False, False).start()

    def chain_wait(b, j):
        @pl.when(j == 4)
        def _():
            chain_copy(b, 0, 4, True, True).wait_recv()
            chain_copy(b, 1, 4, True, True).wait_recv()

        @pl.when((j > 0) & (j < 4))
        def _():
            chain_copy(b, 0, j, False, True).wait_recv()
            chain_copy(b, 1, j, False, True).wait_recv()

    @pl.loop(0, 6)
    def _(i):
        @pl.when(i < 5)
        def _():
            j = 4 - i
            x = pair(0, j)
            PG[...] = nn(x, VG[...])
            ring_step(0, PG, j)
            PU[...] = nn(x, VU[...])
            ring_step(1, PU, j)

            @pl.when(j == 0)
            def _():
                low_wait()
                low = low_chunk(0)
                gate = ring_total(0, PG) + SCALE * nn(half_rows(low, True), BGU[...])
                up = ring_total(1, PU) + SCALE * nn(half_rows(low, False), BGU[...])
                GA[...] = gate
                UA[...] = up
                H[0, z] = (gate * jax.nn.sigmoid(gate) * up).astype(BF16)
                chain_start(0, 1)

        @pl.when(i == 0)
        def _():
            spread_far(1)

        @pl.when(i == 1)
        def _():
            spread_wait(1)

        @pl.when(i == 5)
        def _():
            chain_wait(0, 1)
            chain_start(0, 2)

        @pl.when(i > 0)
        def _():
            j = 5 - i
            PH[...] = nt(pair(1, j), VD[...])
            ring_step(2, PH, j)

            @pl.when(j == 0)
            def _():
                grad = ring_total(2, PH) + SCALE * nn(low_chunk(1)[:, 0:R], AD[...])
                gate, up = GA[...], UA[...]
                sigma = jax.nn.sigmoid(gate)
                H[1, z] = (grad * up * sigma * (1.0 + gate * (1.0 - sigma))).astype(BF16)
                chain_start(1, 1)
                H[2, z] = (grad * gate * sigma).astype(BF16)
                chain_start(2, 1)

        @pl.when(i == 1)
        def _():
            low_sum()

    def sib_copy(f, d):
        rows = pl.ds(pl.multiple_of((1 - c) * 32, 32), 32)
        return remote(ST.at[f, d, rows], SB.at[f, d], sbs.at[f, d], sbr.at[f, d], z, sibling)

    def sib_start(f, j):
        da, db = mod(z + NZ - j, NZ), mod(z + j, NZ)
        sib_copy(f, da).start()

        @pl.when((j > 0) & (j < 4))
        def _():
            sib_copy(f, db).start()

    def owner_copy(f, d, k):
        return remote(
            O2.at[f, d, pl.ds(k * TB, TB)], RX.at[f, q], rxs.at[f, 2 * d + k], rxr.at[f, q],
            z, owner(d, c, k),
        )

    def combine_one(f, d):
        sib_copy(f, d).wait_recv()
        rows = pl.ds(pl.multiple_of(c * 32, 32), 32)
        total = (ST[f, d, rows].astype(F32) + SB[f, d].astype(F32)).astype(BF16)
        O2[f, d] = total
        for k in range(2):
            own = owner(d, c, k) == g

            @pl.when(own)
            def _():
                RX[f, q] = total[k * TB : (k + 1) * TB]

            @pl.when(jnp.logical_not(own))
            def _():
                owner_copy(f, d, k).start()

    def combine(f, j):
        combine_one(f, mod(z + NZ - j, NZ))

        @pl.when((j > 0) & (j < 4))
        def _():
            combine_one(f, mod(z + j, NZ))

    def hpair(b, j):
        return jnp.concatenate([H[b, mod(z + NZ - j, NZ)], H[b, mod(z + j, NZ)]], axis=0)

    def adapter_grads(b, j, x):
        low = jnp.concatenate([LA[p, 0:TB] for d in (mod(z + NZ - j, NZ), mod(z + j, NZ)) for p in owners(d)], axis=0)
        once = (lax.broadcasted_iota(jnp.int32, (2 * CH, 128), 0) < CH) | (mod(j, 4) > 0)
        LOWF[b] += tn(jnp.where(once, low, jnp.zeros_like(low)), x)

    LOWF[...] = jnp.zeros((2, 128, FF), F32)

    def stage(f, j, wide, low, width):
        for n, d in enumerate((mod(z + NZ - j, NZ), mod(z + j, NZ))):
            ST[f, d, :, 0:D] = wide[n * CH : (n + 1) * CH].astype(BF16)
            ST[f, d, :, D : D + width] = low[n * CH : (n + 1) * CH].astype(BF16)

    ST[0, :, :, D + R : W] = jnp.zeros((NZ, CH, R), BF16)

    def rows_total(f):
        @pl.loop(0, NC)
        def _(s):
            @pl.when(s != q)
            def _():
                remote(RX.at[f, s], RX.at[f, s], rxs.at[f, 0], rxr.at[f, s], z, g).wait_recv()

        return jnp.sum(RX[f].astype(F32), axis=0)

    def chain_pass(b, j):
        @pl.when(j > 0)
        def _():
            chain_wait(b, j)

            @pl.when(j < 4)
            def _():
                chain_start(b, j + 1)

    @pl.loop(0, 6)
    def _(u):
        j = u - 1

        @pl.when((u > 1) & (u < 5))
        def _():
            chain_pass(0, u)

        @pl.when(u < 5)
        def _():
            x = hpair(0, u)
            stage(0, u, nn(x, VD[...]), nt(x, AD[...]), R)
            sib_start(0, u)

        @pl.when(j > 0)
        def _():
            combine(1, j - 1)

        @pl.when(j >= 0)
        def _():
            chain_pass(1, j)
            x = hpair(1, j)
            WIDE[:, 0:D] = nt(x, VG[...])
            WIDE[:, D:W] = nt(x, BGU[...])
            adapter_grads(0, j, x)

        @pl.when(u < 5)
        def _():
            combine(0, u)

        @pl.when(u == 5)
        def _():
            total = rows_total(0)
            down_low = total[:, D : D + R].astype(BF16)
            DL[me, :, 0:R] = down_low

            @pl.loop(1, NG)
            def _(k):
                to_plane(DL, dls, dlr, k).start()

            out[...] = (total[:, 0:D] + SCALE * nn(down_low, BD[...])).astype(BF16)

        @pl.when(j >= 0)
        def _():
            chain_pass(2, j)
            x = hpair(2, j)
            lane = lax.broadcasted_iota(jnp.int32, (2 * CH, 128), 1)
            low = jnp.where(lane < R, WIDE[:, D:W], nt(x, BGU[...]))
            stage(1, j, WIDE[:, 0:D] + nt(x, VU[...]), low, 128)
            sib_start(1, j)
            adapter_grads(1, j, x)

    for b, ref in ((0, gmap), (1, umap)):
        ref[...] = SCALE * LOWF[b, pl.ds(pl.multiple_of(R * b + 8 * z, 8), 8)]

    combine(1, 4)

    for a in range(2):
        for i in range(SIDE):
            for k in range(SIDE):
                if k:
                    far(a, me, i, k).wait_send()
                elif i:
                    near(a, me, i).wait_send()
                relay(a, me, i, k).wait_send()

    @pl.loop(1, NZ)
    def _(k):
        remote(LZ.at[z], LZ.at[z], lzs.at[k], lzr.at[k], z, g).wait_send()

    @pl.loop(1, NG)
    def _(k):
        to_plane(LA, las, lar, k).wait_send()

    for a in range(3):
        for way in range(2):
            ring_copy(a, way, 4, True).wait_send()

            @pl.loop(1, 4)
            def _(j):
                ring_copy(a, way, j, False).wait_send()

    @pl.loop(1, NG)
    def _(k):
        from_plane(DL, dls, dlr, k).wait_recv()

    grads = SCALE * tn(DL[...].reshape(NG * TB, 128), X[1].reshape(NG * TB, D))
    rank = lax.broadcasted_iota(jnp.int32, (128, D), 0)
    for k in range(2):
        dmap[k : k + 1] = jnp.sum(jnp.where(rank == 2 * g + k, grads, 0.0), axis=0, keepdims=True)

    total = rows_total(1)
    back = total[:, D:W].astype(BF16)
    tig[...] = (total[:, 0:D] + SCALE * nn(back, AGU[...])).astype(BF16)

    @pl.loop(1, NG)
    def _(k):
        to_plane(DL, dls, dlr, k).wait_send()

    for a in range(3):
        for way in range(2):
            chain_copy(a, way, 4, True, False).wait_send()

            @pl.loop(1, 4)
            def _(j):
                chain_copy(a, way, j, False, False).wait_send()

    @pl.loop(0, NZ)
    def _(d):
        for f in range(2):
            sib_copy(f, d).wait_send()
            for k in range(2):
                @pl.when(owner(d, c, k) != g)
                def _():
                    owner_copy(f, d, k).wait_send()


def place(*refs):
    for a, b in zip(refs[:5], refs[5:]):
        b[...] = a[...]


def body(tok, wg, wu, wd, ag, au, ad, bg, bu, bd, cot):
    dma = pltpu.SemaphoreType.DMA
    hbm = pl.BlockSpec(memory_space=pltpu.HBM)
    vmem = pl.BlockSpec(memory_space=pltpu.VMEM)
    args = (tok, wg, wu, wd, ag.T, au.T, ad.T, bg, bu, bd, cot)
    results = pl.pallas_call(
        kernel,
        out_shape=(
            jax.ShapeDtypeStruct((TB, D), BF16),
            jax.ShapeDtypeStruct((TB, D), BF16),
            jax.ShapeDtypeStruct((8, FF), F32),
            jax.ShapeDtypeStruct((8, FF), F32),
            jax.ShapeDtypeStruct((2, D), F32),
        ),
        in_specs=[hbm] * 11,
        out_specs=(vmem,) * 5,
        scratch_shapes=[
            pltpu.VMEM((2, NG, TB, D), BF16),
            pltpu.VMEM((D, FF), BF16),
            pltpu.VMEM((D, FF), BF16),
            pltpu.VMEM((FF, D), BF16),
            pltpu.VMEM((2 * R, D), BF16),
            pltpu.VMEM((R, FF), BF16),
            pltpu.VMEM((2 * R, FF), BF16),
            pltpu.VMEM((R, D), BF16),
            pltpu.VMEM((NZ, 2 * TB, 128), BF16),
            pltpu.VMEM((NG, 2 * TB, 128), BF16),
            pltpu.VMEM((NG, TB, 128), BF16),
            pltpu.VMEM((2 * CH, FF), F32),
            pltpu.VMEM((2 * CH, FF), F32),
            pltpu.VMEM((2 * CH, FF), F32),
            pltpu.VMEM((2 * CH, W), F32),
            pltpu.VMEM((CH, FF), F32),
            pltpu.VMEM((CH, FF), F32),
            pltpu.VMEM((3, 2, 4, CH, FF), BF16),
            pltpu.VMEM((3, 2, 5, CH, FF), BF16),
            pltpu.VMEM((3, NZ, CH, FF), BF16),
            pltpu.VMEM((2, NZ, CH, W), BF16),
            pltpu.VMEM((2, NZ, CH // 2, W), BF16),
            pltpu.VMEM((2, NZ, CH // 2, W), BF16),
            pltpu.VMEM((2, NC, TB, W), BF16),
            pltpu.VMEM((2, 128, FF), F32),
            dma((9,)),
            dma((2,)),
            dma((2, SIDE)),
            dma((2, SIDE)),
            dma((2, SIDE, SIDE)),
            dma((2, SIDE, SIDE)),
            dma((2, SIDE, SIDE)),
            dma((2, SIDE, SIDE)),
            dma((NZ,)),
            dma((NZ,)),
            dma((NG,)),
            dma((NG,)),
            dma((NG,)),
            dma((NG,)),
            dma((3, 2, 4)),
            dma((3, 2, 4)),
            dma((3, 2, 4)),
            dma((3, 2, 4)),
            dma((2, NZ)),
            dma((2, NZ)),
            dma((2, 2 * NZ)),
            dma((2, NC)),
        ],
        compiler_params=pltpu.CompilerParams(
            collective_id=0, has_side_effects=True, vmem_limit_bytes=VMEM
        ),
    )(*args)
    return pl.pallas_call(
        place,
        out_shape=tuple(jax.ShapeDtypeStruct(r.shape, r.dtype) for r in results),
        in_specs=[vmem] * 5,
        out_specs=(vmem,) * 5,
    )(*results)


def solution(mesh):
    in_specs = (
        P("gy", "gx"),
        P("gx", "gy"),
        P("gx", "gy"),
        P("gy", "gx"),
        P("gx", None),
        P("gx", None),
        P("gy", None),
        P(None, "gy"),
        P(None, "gy"),
        P(None, "gx"),
        P("gy", "gx"),
    )
    out_specs = (P("gy", "gx"), P("gy", "gx"), P("gx", "gy"), P("gx", "gy"), P("gy", "gx"))
    return jax.shard_map(body, mesh=mesh, in_specs=in_specs, out_specs=out_specs, check_vma=False)
```

```python
import functools

import jax
import jax.numpy as jnp
from jax import lax
from jax.experimental import pallas as pl
from jax.experimental.pallas import tpu as pltpu
from jax.sharding import PartitionSpec as P

MESH = pl.DeviceIdType.MESH
F32 = jnp.float32
BF16 = jnp.bfloat16

NZ = 8
NG = 32
SIDE = 4
NC = 16
TB = 16
CH = 64
D = 1024
FF = 896
R = 64
W = D + 128
SCALE = 0.5
VMEM = 60 * 1024 * 1024


def mod(a, m):
    return lax.rem(a, m)


def nn(left, right):
    return jnp.dot(left, right, preferred_element_type=F32)


def nt(left, right):
    return lax.dot_general(left, right, (((1,), (1,)), ((), ())), preferred_element_type=F32)


def tn(left, right):
    return lax.dot_general(left, right, (((0,), (0,)), ((), ())), preferred_element_type=F32)


def kernel(
    tok, wg, wu, wd, ag, au, ad, bg, bu, bd, cot,
    out, tig, gmap, umap, dmap,
    X, VG, VU, VD, AGU, AD, BGU, BD,
    LZ, LA, DL, PS, PG, PU, PH, WIDE, GA, UA, RS, RR, H, ST, SB, O2, RX, LOWF,
    wsem, xsem, xs, xr, vs, vr, ys, yr, lzs, lzr, las, lar, dls, dlr, rss, rsr, ags, agr, sbs, sbr, rxs, rxr,
):
    z = lax.axis_index("gx")
    g = lax.axis_index("gy")
    q, c = lax.div(g, 2), mod(g, 2)
    qx, qy = mod(q, SIDE), lax.div(q, SIDE)
    sibling = g + 1 - 2 * c
    right, left = mod(z + 1, NZ), mod(z + NZ - 1, NZ)

    columns = [2 * mod(qx + i, SIDE) for i in range(SIDE)]
    rows = [8 * mod(qy + i, SIDE) for i in range(SIDE)]
    first = [a + c * (b - a) for a, b in zip(columns, rows)]
    second = [b + c * (a - b) for a, b in zip(columns, rows)]

    def device_at(i, k):
        return first[i % SIDE] + second[k % SIDE] + c

    def sibling_at(i, k):
        return second[i % SIDE] + first[k % SIDE] + 1 - c

    def gray(n):
        return n + lax.div(n, 2) * (1 - 2 * mod(n, 2))

    def place_of(d, n):
        return 2 * mod(d + n, 2) + lax.div(n, 2)

    def device_of(d, n):
        t, step, cc = lax.div(d, 2), gray(n), mod(d + n, 2)
        across, along = 2 * t + 8 * mod(qy + step, SIDE), 2 * mod(qx + step, SIDE) + 8 * t + 1
        return across + cc * (along - across)

    def owner(d, cc, k):
        return device_of(d, 2 * k + mod(d + cc, 2))

    def remote(src, dst, ssem, rsem, zz, gg):
        return pltpu.make_async_remote_copy(
            src_ref=src, dst_ref=dst, send_sem=ssem, recv_sem=rsem, device_id=(zz, gg), device_id_type=MESH
        )

    me = g

    barrier = pltpu.get_barrier_semaphore()

    @pl.loop(1, NG)
    def _(k):
        pl.semaphore_signal(barrier, inc=1, device_id=(z, mod(g + k, NG)), device_id_type=MESH)

    @pl.loop(1, NZ)
    def _(k):
        pl.semaphore_signal(barrier, inc=1, device_id=(mod(z + k, NZ), g), device_id_type=MESH)

    own_copies = [
        pltpu.make_async_copy(tok, X.at[0, me], xsem.at[0]),
        pltpu.make_async_copy(cot, X.at[1, me], xsem.at[1]),
    ]
    low_copies = [
        pltpu.make_async_copy(ag, AGU.at[pl.ds(0, R)], wsem.at[0]),
        pltpu.make_async_copy(au, AGU.at[pl.ds(R, R)], wsem.at[1]),
        pltpu.make_async_copy(bd, BD, wsem.at[2]),
    ]
    gate_copies = [
        pltpu.make_async_copy(wg, VG, wsem.at[3]),
        pltpu.make_async_copy(wu, VU, wsem.at[4]),
    ]
    rest_copies = [
        pltpu.make_async_copy(wd, VD, wsem.at[5]),
        pltpu.make_async_copy(ad, AD, wsem.at[6]),
        pltpu.make_async_copy(bg, BGU.at[pl.ds(0, R)], wsem.at[7]),
        pltpu.make_async_copy(bu, BGU.at[pl.ds(R, R)], wsem.at[8]),
    ]
    for copy in own_copies + low_copies + gate_copies + rest_copies:
        copy.start()

    pl.semaphore_wait(barrier, NG - 1 + NZ - 1)

    def held(a, s):
        return (tok, cot)[a] if s is me else X.at[a, s]

    def near(a, s, i):
        return remote(held(a, s), X.at[a, s], xs.at[a, i], xr.at[a, i], z, device_at(i, 0))

    def far(a, s, i, k):
        return remote(held(a, s), X.at[a, s], vs.at[a, i, k], vr.at[a, i, k], z, device_at(0, k))

    def relay(a, s, i, k):
        return remote(held(a, s), X.at[a, s], ys.at[a, i, k], yr.at[a, i, k], z, sibling)

    def spread_near(a):
        for i in (1, 3, 2):
            near(a, me, i).start()

    def spread_own(a):
        for k in (1, 3, 2):
            far(a, me, 0, k).start()
        relay(a, me, 0, 0).start()

    def spread_turn(a):
        for i in (1, 3, 2):
            s = device_at(-i, 0)
            near(a, s, i).wait_recv()
            for k in (1, 3, 2):
                far(a, s, i, k).start()
            relay(a, s, i, 0).start()

    def spread_far(a):
        for k in (3, 1, 2):
            for i in (0, 1, 3, 2):
                s = device_at(-i, -k)
                far(a, s, i, k).wait_recv()
                relay(a, s, i, k).start()

    def spread_wait(a, steps):
        for k in steps:
            for i in (0, 1, 3, 2):
                relay(a, sibling_at(-i, -k), i, k).wait_recv()

    spread_near(0)
    spread_own(0)
    spread_near(1)

    RR[:, 0, 3, 2:4] = jnp.zeros((3, 2, TB, FF), BF16)
    RR[:, 1, 3, 0:2] = jnp.zeros((3, 2, TB, FF), BF16)
    RR[:, :, 4] = jnp.zeros((3, 2, 4, TB, FF), BF16)
    LZ[z] = jnp.zeros((2 * TB, 128), BF16)
    DL[me] = jnp.zeros((TB, 128), BF16)

    for copy in own_copies:
        copy.wait()

    for copy in low_copies:
        copy.wait()
    LZ[z, 0:TB] = nt(X[0, me], AGU[...]).astype(BF16)
    LZ[z, TB : 2 * TB, 0:R] = nt(X[1, me], BD[...]).astype(BF16)

    @pl.loop(1, NZ)
    def _(k):
        remote(LZ.at[z], LZ.at[z], lzs.at[k], lzr.at[k], mod(z + k, NZ), g).start()

    spread_turn(0)
    spread_own(1)

    def to_plane(ref, ssem, rsem, k):
        return remote(ref.at[me], ref.at[me], ssem.at[k], rsem.at[k], z, mod(g + k, NG))

    def from_plane(ref, ssem, rsem, k):
        s = mod(g + NG - k, NG)
        return remote(ref.at[s], ref.at[s], ssem.at[k], rsem.at[k], z, g)

    def low_sum():
        @pl.loop(1, NZ)
        def _(k):
            s = mod(z + NZ - k, NZ)
            remote(LZ.at[s], LZ.at[s], lzs.at[k], lzr.at[k], z, g).wait_recv()

        LA[me] = jnp.sum(LZ[...].astype(F32), axis=0).astype(BF16)

        @pl.loop(1, NG)
        def _(k):
            to_plane(LA, las, lar, k).start()

    def low_wait():
        @pl.loop(1, NG)
        def _(k):
            from_plane(LA, las, lar, k).wait_recv()

    def ring_copy(a, way, j, far):
        at, size = (1, 3) if far else (0, 1)
        if far and isinstance(j, int) and j == 4:
            at, size = (2, 2) if way else (1, 1)
        blocks = pl.ds(at, size)
        level = far * 4 + j - 1
        return remote(
            RS.at[a, way, j - 1, blocks], RR.at[a, way, j - 1, blocks],
            rss.at[a, way, level], rsr.at[a, way, level], left if way else right, g,
        )

    def ring_wait(a, j, far):
        @pl.when(j == 3)
        def _():
            ring_copy(a, 0, 4, far).wait_recv()
            if far:
                ring_copy(a, 1, 4, far).wait_recv()

        @pl.when(j < 3)
        def _():
            ring_copy(a, 0, j + 1, far).wait_recv()
            ring_copy(a, 1, j + 1, far).wait_recv()

    def ring_send(a, j, far):
        @pl.when(j == 4)
        def _():
            ring_copy(a, 0, 4, far).start()
            if far:
                ring_copy(a, 1, 4, far).start()

        @pl.when((j > 0) & (j < 4))
        def _():
            ring_copy(a, 0, j, far).start()
            ring_copy(a, 1, j, far).start()

    def near_products(a, x, weight):
        PS[a] = weight(x).reshape(NZ, TB, FF)
        RS[a, 0, 3, 0] = PS[a, mod(z + 4, NZ)].astype(BF16)
        ring_copy(a, 0, 4, False).start()

    def near_step(a, j):
        ring_wait(a, j, False)

        @pl.when(j > 0)
        def _():
            for way, d in ((0, mod(z + j, NZ)), (1, mod(z + NZ - j, NZ))):
                RS[a, way, j - 1, 0] = (PS[a, d] + RR[a, way, j, 0].astype(F32)).astype(BF16)

        ring_send(a, j, False)

    def near_group(a):
        return jnp.concatenate([X[a, device_of(d, 0)] for d in range(NZ)], axis=0)

    def pair(a, j):
        chunks = (mod(z + j, NZ), mod(z + NZ - j, NZ))
        return jnp.concatenate([X[a, device_of(d, n)] for d in chunks for n in (1, 2, 3)], axis=0)

    def ring_step(a, part, j):
        ring_wait(a, j, True)

        @pl.when(j > 0)
        def _():
            for way in range(2):
                total = part[way * 3 * TB : (way + 1) * 3 * TB].reshape(3, TB, FF) + RR[a, way, j, 1:4].astype(F32)
                RS[a, way, j - 1, 1:4] = total.astype(BF16)

        ring_send(a, j, True)

    def ring_total(a, part):
        own = jnp.concatenate([PS[a, z], part[0 : 3 * TB]], axis=0)
        return own + (RR[a, 0, 0].astype(F32) + RR[a, 1, 0].astype(F32)).reshape(CH, FF)

    def low_chunk(which):
        return jnp.concatenate([LA[device_of(z, n), which * TB : (which + 1) * TB] for n in range(4)], axis=0)

    def put_chunk(b, value):
        for n in range(4):
            H[b, z, place_of(z, n)] = value[n * TB : (n + 1) * TB].astype(BF16)

    def half_rows(low, first):
        lane = lax.broadcasted_iota(jnp.int32, low.shape, 1)
        return jnp.where((lane < R) == first, low, jnp.zeros_like(low))

    def chain_copy(b, way, j, half, arriving):
        hops = j if arriving else j - 1
        d = mod(z + hops, NZ) if way else mod(z + NZ - hops, NZ)
        blocks = pl.ds(2 * way, 2) if half else pl.ds(0, 4)
        return remote(
            H.at[b, d, blocks], H.at[b, d, blocks],
            ags.at[b, way, j - 1], agr.at[b, way, j - 1], left if way else right, g,
        )

    def chain_start(b, j):
        @pl.when(j == 4)
        def _():
            chain_copy(b, 0, 4, True, False).start()
            chain_copy(b, 1, 4, True, False).start()

        @pl.when(j < 4)
        def _():
            chain_copy(b, 0, j, False, False).start()
            chain_copy(b, 1, j, False, False).start()

    def chain_wait(b, j):
        @pl.when(j == 4)
        def _():
            chain_copy(b, 0, 4, True, True).wait_recv()
            chain_copy(b, 1, 4, True, True).wait_recv()

        @pl.when((j > 0) & (j < 4))
        def _():
            chain_copy(b, 0, j, False, True).wait_recv()
            chain_copy(b, 1, j, False, True).wait_recv()

    spread_wait(0, (0,))
    for copy in gate_copies:
        copy.wait()
    x = near_group(0)
    near_products(0, x, lambda x: nn(x, VG[...]))
    near_products(1, x, lambda x: nn(x, VU[...]))
    spread_turn(1)
    spread_wait(1, (0,))
    for copy in rest_copies:
        copy.wait()
    near_products(2, near_group(1), lambda x: nt(x, VD[...]))
    spread_far(0)

    @pl.loop(0, 2)
    def _(a):
        near_step(a, 3)

    spread_wait(0, (3, 1, 2))

    @pl.loop(0, 6)
    def _(i):
        @pl.when(i < 5)
        def _():
            j = 4 - i
            x = pair(0, j)
            PG[...] = nn(x, VG[...])
            ring_step(0, PG, j)
            PU[...] = nn(x, VU[...])
            ring_step(1, PU, j)

            @pl.when(j == 0)
            def _():
                low_wait()
                low = low_chunk(0)
                gate = ring_total(0, PG) + SCALE * nn(half_rows(low, True), BGU[...])
                up = ring_total(1, PU) + SCALE * nn(half_rows(low, False), BGU[...])
                GA[...] = gate
                UA[...] = up
                put_chunk(0, gate * jax.nn.sigmoid(gate) * up)
                chain_start(0, 1)

        @pl.when(i < 3)
        def _():
            near_step(0, 2 - i)
            near_step(1, 2 - i)

        @pl.when(i < 4)
        def _():
            near_step(2, 3 - i)

        @pl.when(i == 0)
        def _():
            spread_far(1)

        @pl.when(i == 1)
        def _():
            spread_wait(1, (3, 1, 2))

        @pl.when(i == 5)
        def _():
            chain_wait(0, 1)
            chain_start(0, 2)

        @pl.when(i > 0)
        def _():
            j = 5 - i
            PH[...] = nt(pair(1, j), VD[...])
            ring_step(2, PH, j)

            @pl.when(j == 0)
            def _():
                grad = ring_total(2, PH) + SCALE * nn(low_chunk(1)[:, 0:R], AD[...])
                gate, up = GA[...], UA[...]
                sigma = jax.nn.sigmoid(gate)
                put_chunk(1, grad * up * sigma * (1.0 + gate * (1.0 - sigma)))
                chain_start(1, 1)
                put_chunk(2, grad * gate * sigma)
                chain_start(2, 1)

        @pl.when(i == 1)
        def _():
            low_sum()

    def sib_copy(f, d):
        rows = pl.ds(pl.multiple_of((1 - c) * 32, 32), 32)
        return remote(ST.at[f, d, rows], SB.at[f, d], sbs.at[f, d], sbr.at[f, d], z, sibling)

    def sib_start(f, j):
        da, db = mod(z + NZ - j, NZ), mod(z + j, NZ)
        sib_copy(f, da).start()

        @pl.when((j > 0) & (j < 4))
        def _():
            sib_copy(f, db).start()

    def owner_copy(f, d, k):
        return remote(
            O2.at[f, d, pl.ds(k * TB, TB)], RX.at[f, q], rxs.at[f, 2 * d + k], rxr.at[f, q],
            z, owner(d, c, k),
        )

    def combine_one(f, d):
        sib_copy(f, d).wait_recv()
        rows = pl.ds(pl.multiple_of(c * 32, 32), 32)
        total = (ST[f, d, rows].astype(F32) + SB[f, d].astype(F32)).astype(BF16)
        O2[f, d] = total
        for k in range(2):
            own = owner(d, c, k) == g

            @pl.when(own)
            def _():
                RX[f, q] = total[k * TB : (k + 1) * TB]

            @pl.when(jnp.logical_not(own))
            def _():
                owner_copy(f, d, k).start()

    def combine(f, j):
        combine_one(f, mod(z + NZ - j, NZ))

        @pl.when((j > 0) & (j < 4))
        def _():
            combine_one(f, mod(z + j, NZ))

    def hpair(b, j):
        return jnp.concatenate([H[b, d].reshape(CH, FF) for d in (mod(z + NZ - j, NZ), mod(z + j, NZ))], axis=0)

    def adapter_grads(b, j, x):
        da, db = mod(z + NZ - j, NZ), mod(z + j, NZ)
        low = [LA[device_of(d, n), 0:TB] for d in (da, db) for n in (0, 2, 1, 3)]
        low = [jnp.where(mod(d, 2) == 0, low[4 * m + i], low[4 * m + (i + 2) % 4]) for m, d in enumerate((da, db)) for i in range(4)]
        low = jnp.concatenate(low, axis=0)
        once = (lax.broadcasted_iota(jnp.int32, (2 * CH, 128), 0) < CH) | (mod(j, 4) > 0)
        LOWF[b] += tn(jnp.where(once, low, jnp.zeros_like(low)), x)

    LOWF[...] = jnp.zeros((2, 128, FF), F32)

    def stage(f, j, wide, low, width):
        for n, d in enumerate((mod(z + NZ - j, NZ), mod(z + j, NZ))):
            ST[f, d, :, 0:D] = wide[n * CH : (n + 1) * CH].astype(BF16)
            ST[f, d, :, D : D + width] = low[n * CH : (n + 1) * CH].astype(BF16)

    ST[0, :, :, D + R : W] = jnp.zeros((NZ, CH, R), BF16)

    def rows_total(f):
        @pl.loop(0, NC)
        def _(s):
            @pl.when(s != q)
            def _():
                remote(RX.at[f, s], RX.at[f, s], rxs.at[f, 0], rxr.at[f, s], z, g).wait_recv()

        return jnp.sum(RX[f].astype(F32), axis=0)

    def chain_pass(b, j):
        @pl.when(j > 0)
        def _():
            chain_wait(b, j)

            @pl.when(j < 4)
            def _():
                chain_start(b, j + 1)

    @pl.loop(0, 6)
    def _(u):
        j = u - 1

        @pl.when((u > 1) & (u < 5))
        def _():
            chain_pass(0, u)

        @pl.when(u < 5)
        def _():
            x = hpair(0, u)
            stage(0, u, nn(x, VD[...]), nt(x, AD[...]), R)
            sib_start(0, u)

        @pl.when(j > 0)
        def _():
            combine(1, j - 1)

        @pl.when(j >= 0)
        def _():
            chain_pass(1, j)
            x = hpair(1, j)
            WIDE[:, 0:D] = nt(x, VG[...])
            WIDE[:, D:W] = nt(x, BGU[...])
            adapter_grads(0, j, x)

        @pl.when(u < 5)
        def _():
            combine(0, u)

        @pl.when(u == 5)
        def _():
            total = rows_total(0)
            down_low = total[:, D : D + R].astype(BF16)
            DL[me, :, 0:R] = down_low

            @pl.loop(1, NG)
            def _(k):
                to_plane(DL, dls, dlr, k).start()

            out[...] = (total[:, 0:D] + SCALE * nn(down_low, BD[...])).astype(BF16)

        @pl.when(j >= 0)
        def _():
            chain_pass(2, j)
            x = hpair(2, j)
            lane = lax.broadcasted_iota(jnp.int32, (2 * CH, 128), 1)
            low = jnp.where(lane < R, WIDE[:, D:W], nt(x, BGU[...]))
            stage(1, j, WIDE[:, 0:D] + nt(x, VU[...]), low, 128)
            sib_start(1, j)
            adapter_grads(1, j, x)

    for b, ref in ((0, gmap), (1, umap)):
        ref[...] = SCALE * LOWF[b, pl.ds(pl.multiple_of(R * b + 8 * z, 8), 8)]

    combine(1, 4)

    for a in range(2):
        for i in range(SIDE):
            for k in range(SIDE):
                if k:
                    far(a, me, i, k).wait_send()
                elif i:
                    near(a, me, i).wait_send()
                relay(a, me, i, k).wait_send()

    @pl.loop(1, NZ)
    def _(k):
        remote(LZ.at[z], LZ.at[z], lzs.at[k], lzr.at[k], z, g).wait_send()

    @pl.loop(1, NG)
    def _(k):
        to_plane(LA, las, lar, k).wait_send()

    for a in range(3):
        ring_copy(a, 0, 4, False).wait_send()
        for way in range(2):
            ring_copy(a, way, 4, True).wait_send()
            for j in range(1, 4):
                ring_copy(a, way, j, True).wait_send()
                ring_copy(a, way, j, False).wait_send()

    @pl.loop(1, NG)
    def _(k):
        from_plane(DL, dls, dlr, k).wait_recv()

    grads = SCALE * tn(DL[...].reshape(NG * TB, 128), X[1].reshape(NG * TB, D))
    rank = lax.broadcasted_iota(jnp.int32, (128, D), 0)
    for k in range(2):
        dmap[k : k + 1] = jnp.sum(jnp.where(rank == 2 * g + k, grads, 0.0), axis=0, keepdims=True)

    @pl.loop(1, NG)
    def _(k):
        to_plane(DL, dls, dlr, k).wait_send()

    for a in range(3):
        for way in range(2):
            chain_copy(a, way, 4, True, False).wait_send()
            for j in range(1, 4):
                chain_copy(a, way, j, False, False).wait_send()

    def owner_sent(f, d):
        for k in range(2):
            @pl.when(owner(d, c, k) != g)
            def _():
                owner_copy(f, d, k).wait_send()

    @pl.loop(0, NZ)
    def _(d):
        for f in range(2):
            sib_copy(f, d).wait_send()
        owner_sent(0, d)

        @pl.when(d != mod(z + 4, NZ))
        def _():
            owner_sent(1, d)

    total = rows_total(1)
    back = total[:, D:W].astype(BF16)
    tig[...] = (total[:, 0:D] + SCALE * nn(back, AGU[...])).astype(BF16)
    owner_sent(1, mod(z + 4, NZ))


def place(*refs):
    for a, b in zip(refs[:5], refs[5:]):
        b[...] = a[...]


def body(tok, wg, wu, wd, ag, au, ad, bg, bu, bd, cot):
    dma = pltpu.SemaphoreType.DMA
    hbm = pl.BlockSpec(memory_space=pltpu.HBM)
    vmem = pl.BlockSpec(memory_space=pltpu.VMEM)
    args = (tok, wg, wu, wd, ag.T, au.T, ad.T, bg, bu, bd, cot)
    results = pl.pallas_call(
        kernel,
        out_shape=(
            jax.ShapeDtypeStruct((TB, D), BF16),
            jax.ShapeDtypeStruct((TB, D), BF16),
            jax.ShapeDtypeStruct((8, FF), F32),
            jax.ShapeDtypeStruct((8, FF), F32),
            jax.ShapeDtypeStruct((2, D), F32),
        ),
        in_specs=[hbm] * 11,
        out_specs=(vmem,) * 5,
        scratch_shapes=[
            pltpu.VMEM((2, NG, TB, D), BF16),
            pltpu.VMEM((D, FF), BF16),
            pltpu.VMEM((D, FF), BF16),
            pltpu.VMEM((FF, D), BF16),
            pltpu.VMEM((2 * R, D), BF16),
            pltpu.VMEM((R, FF), BF16),
            pltpu.VMEM((2 * R, FF), BF16),
            pltpu.VMEM((R, D), BF16),
            pltpu.VMEM((NZ, 2 * TB, 128), BF16),
            pltpu.VMEM((NG, 2 * TB, 128), BF16),
            pltpu.VMEM((NG, TB, 128), BF16),
            pltpu.VMEM((3, NZ, TB, FF), F32),
            pltpu.VMEM((6 * TB, FF), F32),
            pltpu.VMEM((6 * TB, FF), F32),
            pltpu.VMEM((6 * TB, FF), F32),
            pltpu.VMEM((2 * CH, W), F32),
            pltpu.VMEM((CH, FF), F32),
            pltpu.VMEM((CH, FF), F32),
            pltpu.VMEM((3, 2, 4, 4, TB, FF), BF16),
            pltpu.VMEM((3, 2, 5, 4, TB, FF), BF16),
            pltpu.VMEM((3, NZ, 4, TB, FF), BF16),
            pltpu.VMEM((2, NZ, CH, W), BF16),
            pltpu.VMEM((2, NZ, CH // 2, W), BF16),
            pltpu.VMEM((2, NZ, CH // 2, W), BF16),
            pltpu.VMEM((2, NC, TB, W), BF16),
            pltpu.VMEM((2, 128, FF), F32),
            dma((9,)),
            dma((2,)),
            dma((2, SIDE)),
            dma((2, SIDE)),
            dma((2, SIDE, SIDE)),
            dma((2, SIDE, SIDE)),
            dma((2, SIDE, SIDE)),
            dma((2, SIDE, SIDE)),
            dma((NZ,)),
            dma((NZ,)),
            dma((NG,)),
            dma((NG,)),
            dma((NG,)),
            dma((NG,)),
            dma((3, 2, 8)),
            dma((3, 2, 8)),
            dma((3, 2, 4)),
            dma((3, 2, 4)),
            dma((2, NZ)),
            dma((2, NZ)),
            dma((2, 2 * NZ)),
            dma((2, NC)),
        ],
        compiler_params=pltpu.CompilerParams(
            collective_id=0, has_side_effects=True, vmem_limit_bytes=VMEM
        ),
    )(*args)
    return pl.pallas_call(
        place,
        out_shape=tuple(jax.ShapeDtypeStruct(r.shape, r.dtype) for r in results),
        in_specs=[vmem] * 5,
        out_specs=(vmem,) * 5,
    )(*results)


def solution(mesh):
    in_specs = (
        P("gy", "gx"),
        P("gx", "gy"),
        P("gx", "gy"),
        P("gy", "gx"),
        P("gx", None),
        P("gx", None),
        P("gy", None),
        P(None, "gy"),
        P(None, "gy"),
        P(None, "gx"),
        P("gy", "gx"),
    )
    out_specs = (P("gy", "gx"), P("gy", "gx"), P("gx", "gy"), P("gx", "gy"), P("gy", "gx"))
    return jax.shard_map(body, mesh=mesh, in_specs=in_specs, out_specs=out_specs, check_vma=False)
```

```python
import functools

import jax
import jax.numpy as jnp
from jax import lax
from jax.experimental import pallas as pl
from jax.experimental.pallas import tpu as pltpu
from jax.sharding import PartitionSpec as P

MESH = pl.DeviceIdType.MESH
F32 = jnp.float32
BF16 = jnp.bfloat16

NZ = 8
NG = 32
SIDE = 4
NC = 16
TB = 16
CH = 64
D = 1024
FF = 896
R = 64
W = D + 128
SCALE = 0.5
VMEM = 60 * 1024 * 1024


def mod(a, m):
    return lax.rem(a, m)


def nn(left, right):
    return jnp.dot(left, right, preferred_element_type=F32)


def nt(left, right):
    return lax.dot_general(left, right, (((1,), (1,)), ((), ())), preferred_element_type=F32)


def tn(left, right):
    return lax.dot_general(left, right, (((0,), (0,)), ((), ())), preferred_element_type=F32)


def kernel(
    tok, wg, wu, wd, ag, au, ad, bg, bu, bd, cot,
    out, tig, gmap, umap, dmap,
    X, VG, VU, VD, AGU, AD, BGU, BD,
    LZ, LA, DL, PS, PG, PU, PH, WIDE, GA, UA, RS, RR, H, ST, SB, O2, RX, LOWF,
    wsem, xsem, xs, xr, vs, vr, ys, yr, lzs, lzr, las, lar, dls, dlr, rss, rsr, ags, agr, sbs, sbr, rxs, rxr,
):
    z = lax.axis_index("gx")
    g = lax.axis_index("gy")
    q, c = lax.div(g, 2), mod(g, 2)
    qx, qy = mod(q, SIDE), lax.div(q, SIDE)
    sibling = g + 1 - 2 * c
    right, left = mod(z + 1, NZ), mod(z + NZ - 1, NZ)

    columns = [2 * mod(qx + i, SIDE) for i in range(SIDE)]
    rows = [8 * mod(qy + i, SIDE) for i in range(SIDE)]
    first = [a + c * (b - a) for a, b in zip(columns, rows)]
    second = [b + c * (a - b) for a, b in zip(columns, rows)]

    def device_at(i, k):
        return first[i % SIDE] + second[k % SIDE] + c

    def sibling_at(i, k):
        return second[i % SIDE] + first[k % SIDE] + 1 - c

    def gray(n):
        return n + lax.div(n, 2) * (1 - 2 * mod(n, 2))

    def place_of(d, n):
        return 2 * mod(d + n, 2) + lax.div(n, 2)

    def device_of(d, n):
        t, step, cc = lax.div(d, 2), gray(n), mod(d + n, 2)
        across, along = 2 * t + 8 * mod(qy + step, SIDE), 2 * mod(qx + step, SIDE) + 8 * t + 1
        return across + cc * (along - across)

    def owner(d, cc, k):
        return device_of(d, 2 * k + mod(d + cc, 2))

    def remote(src, dst, ssem, rsem, zz, gg):
        return pltpu.make_async_remote_copy(
            src_ref=src, dst_ref=dst, send_sem=ssem, recv_sem=rsem, device_id=(zz, gg), device_id_type=MESH
        )

    me = g

    barrier = pltpu.get_barrier_semaphore()

    partners = [sibling] + [device_at(i, 0) for i in (1, 2, 3)] + [device_at(0, k) for k in (1, 2, 3)]
    for p in partners:
        pl.semaphore_signal(barrier, inc=1, device_id=(z, p), device_id_type=MESH)

    @pl.loop(1, NZ)
    def _(k):
        pl.semaphore_signal(barrier, inc=1, device_id=(mod(z + k, NZ), g), device_id_type=MESH)

    own_copies = [
        pltpu.make_async_copy(tok, X.at[0, me], xsem.at[0]),
        pltpu.make_async_copy(cot, X.at[1, me], xsem.at[1]),
    ]
    low_copies = [
        pltpu.make_async_copy(ag, AGU.at[pl.ds(0, R)], wsem.at[0]),
        pltpu.make_async_copy(au, AGU.at[pl.ds(R, R)], wsem.at[1]),
        pltpu.make_async_copy(bd, BD, wsem.at[2]),
    ]
    gate_copies = [
        pltpu.make_async_copy(wg, VG, wsem.at[3]),
        pltpu.make_async_copy(wu, VU, wsem.at[4]),
    ]
    rest_copies = [
        pltpu.make_async_copy(wd, VD, wsem.at[5]),
        pltpu.make_async_copy(ad, AD, wsem.at[6]),
        pltpu.make_async_copy(bg, BGU.at[pl.ds(0, R)], wsem.at[7]),
        pltpu.make_async_copy(bu, BGU.at[pl.ds(R, R)], wsem.at[8]),
    ]
    for copy in own_copies + low_copies + gate_copies + rest_copies:
        copy.start()

    pl.semaphore_wait(barrier, len(partners) + NZ - 1)

    def held(a, s):
        return (tok, cot)[a] if s is me else X.at[a, s]

    def near(a, s, i):
        return remote(held(a, s), X.at[a, s], xs.at[a, i], xr.at[a, i], z, device_at(i, 0))

    def far(a, s, i, k):
        return remote(held(a, s), X.at[a, s], vs.at[a, i, k], vr.at[a, i, k], z, device_at(0, k))

    def relay(a, s, i, k):
        return remote(held(a, s), X.at[a, s], ys.at[a, i, k], yr.at[a, i, k], z, sibling)

    def spread_near(a):
        for i in (1, 3, 2):
            near(a, me, i).start()

    def spread_own(a):
        for k in (1, 3, 2):
            far(a, me, 0, k).start()
        relay(a, me, 0, 0).start()

    def spread_turn(a):
        for i in (1, 3, 2):
            s = device_at(-i, 0)
            near(a, s, i).wait_recv()
            for k in (1, 3, 2):
                far(a, s, i, k).start()
            relay(a, s, i, 0).start()

    def spread_far(a):
        for k in (3, 1, 2):
            for i in (0, 1, 3, 2):
                s = device_at(-i, -k)
                far(a, s, i, k).wait_recv()
                relay(a, s, i, k).start()

    def spread_wait(a, steps):
        for k in steps:
            for i in (0, 1, 3, 2):
                relay(a, sibling_at(-i, -k), i, k).wait_recv()

    spread_near(0)
    spread_own(0)
    spread_near(1)

    RR[:, 0, 3, 2:4] = jnp.zeros((3, 2, TB, FF), BF16)
    RR[:, 1, 3, 0:2] = jnp.zeros((3, 2, TB, FF), BF16)
    RR[:, :, 4] = jnp.zeros((3, 2, 4, TB, FF), BF16)
    LZ[z] = jnp.zeros((2 * TB, 128), BF16)
    DL[me] = jnp.zeros((TB, 128), BF16)

    for copy in own_copies:
        copy.wait()

    for copy in low_copies:
        copy.wait()
    LZ[z, 0:TB] = nt(X[0, me], AGU[...]).astype(BF16)
    LZ[z, TB : 2 * TB, 0:R] = nt(X[1, me], BD[...]).astype(BF16)

    @pl.loop(1, NZ)
    def _(k):
        remote(LZ.at[z], LZ.at[z], lzs.at[k], lzr.at[k], mod(z + k, NZ), g).start()

    spread_turn(0)
    spread_own(1)

    def to_plane(ref, ssem, rsem, k):
        return remote(ref.at[me], ref.at[me], ssem.at[k], rsem.at[k], z, mod(g + k, NG))

    def from_plane(ref, ssem, rsem, k):
        s = mod(g + NG - k, NG)
        return remote(ref.at[s], ref.at[s], ssem.at[k], rsem.at[k], z, g)

    def low_sum():
        @pl.loop(1, NZ)
        def _(k):
            s = mod(z + NZ - k, NZ)
            remote(LZ.at[s], LZ.at[s], lzs.at[k], lzr.at[k], z, g).wait_recv()

        LA[me] = jnp.sum(LZ[...].astype(F32), axis=0).astype(BF16)

        @pl.loop(1, NG)
        def _(k):
            to_plane(LA, las, lar, k).start()

    def low_wait():
        @pl.loop(1, NG)
        def _(k):
            from_plane(LA, las, lar, k).wait_recv()

    def ring_copy(a, way, j, far):
        at, size = (1, 3) if far else (0, 1)
        if far and isinstance(j, int) and j == 4:
            at, size = (2, 2) if way else (1, 1)
        blocks = pl.ds(at, size)
        level = far * 4 + j - 1
        return remote(
            RS.at[a, way, j - 1, blocks], RR.at[a, way, j - 1, blocks],
            rss.at[a, way, level], rsr.at[a, way, level], left if way else right, g,
        )

    def ring_wait(a, j, far):
        @pl.when(j == 3)
        def _():
            ring_copy(a, 0, 4, far).wait_recv()
            if far:
                ring_copy(a, 1, 4, far).wait_recv()

        @pl.when(j < 3)
        def _():
            ring_copy(a, 0, j + 1, far).wait_recv()
            ring_copy(a, 1, j + 1, far).wait_recv()

    def ring_send(a, j, far):
        @pl.when(j == 4)
        def _():
            ring_copy(a, 0, 4, far).start()
            if far:
                ring_copy(a, 1, 4, far).start()

        @pl.when((j > 0) & (j < 4))
        def _():
            ring_copy(a, 0, j, far).start()
            ring_copy(a, 1, j, far).start()

    def near_products(a, x, weight):
        PS[a] = weight(x).reshape(NZ, TB, FF)
        RS[a, 0, 3, 0] = PS[a, mod(z + 4, NZ)].astype(BF16)
        ring_copy(a, 0, 4, False).start()

    def near_step(a, j):
        ring_wait(a, j, False)

        @pl.when(j > 0)
        def _():
            for way, d in ((0, mod(z + j, NZ)), (1, mod(z + NZ - j, NZ))):
                RS[a, way, j - 1, 0] = (PS[a, d] + RR[a, way, j, 0].astype(F32)).astype(BF16)

        ring_send(a, j, False)

    def near_group(a):
        return jnp.concatenate([X[a, device_of(d, 0)] for d in range(NZ)], axis=0)

    def pair(a, j):
        chunks = (mod(z + j, NZ), mod(z + NZ - j, NZ))
        return jnp.concatenate([X[a, device_of(d, n)] for d in chunks for n in (1, 2, 3)], axis=0)

    def ring_step(a, part, j):
        ring_wait(a, j, True)

        @pl.when(j > 0)
        def _():
            for way in range(2):
                total = part[way * 3 * TB : (way + 1) * 3 * TB].reshape(3, TB, FF) + RR[a, way, j, 1:4].astype(F32)
                RS[a, way, j - 1, 1:4] = total.astype(BF16)

        ring_send(a, j, True)

    def ring_total(a, part):
        own = jnp.concatenate([PS[a, z], part[0 : 3 * TB]], axis=0)
        return own + (RR[a, 0, 0].astype(F32) + RR[a, 1, 0].astype(F32)).reshape(CH, FF)

    def low_chunk(which):
        return jnp.concatenate([LA[device_of(z, n), which * TB : (which + 1) * TB] for n in range(4)], axis=0)

    def put_chunk(b, value):
        for n in range(4):
            H[b, z, place_of(z, n)] = value[n * TB : (n + 1) * TB].astype(BF16)

    def half_rows(low, first):
        lane = lax.broadcasted_iota(jnp.int32, low.shape, 1)
        return jnp.where((lane < R) == first, low, jnp.zeros_like(low))

    def chain_copy(b, way, j, half, arriving):
        hops = j if arriving else j - 1
        d = mod(z + hops, NZ) if way else mod(z + NZ - hops, NZ)
        blocks = pl.ds(2 * way, 2) if half else pl.ds(0, 4)
        return remote(
            H.at[b, d, blocks], H.at[b, d, blocks],
            ags.at[b, way, j - 1], agr.at[b, way, j - 1], left if way else right, g,
        )

    def chain_start(b, j):
        @pl.when(j == 4)
        def _():
            chain_copy(b, 0, 4, True, False).start()
            chain_copy(b, 1, 4, True, False).start()

        @pl.when(j < 4)
        def _():
            chain_copy(b, 0, j, False, False).start()
            chain_copy(b, 1, j, False, False).start()

    def chain_wait(b, j):
        @pl.when(j == 4)
        def _():
            chain_copy(b, 0, 4, True, True).wait_recv()
            chain_copy(b, 1, 4, True, True).wait_recv()

        @pl.when((j > 0) & (j < 4))
        def _():
            chain_copy(b, 0, j, False, True).wait_recv()
            chain_copy(b, 1, j, False, True).wait_recv()

    spread_wait(0, (0,))
    for copy in gate_copies:
        copy.wait()
    x = near_group(0)
    near_products(0, x, lambda x: nn(x, VG[...]))
    near_products(1, x, lambda x: nn(x, VU[...]))
    spread_turn(1)
    spread_wait(1, (0,))
    for copy in rest_copies:
        copy.wait()
    near_products(2, near_group(1), lambda x: nt(x, VD[...]))
    spread_far(0)

    @pl.loop(0, 2)
    def _(a):
        near_step(a, 3)

    spread_wait(0, (3, 1, 2))

    @pl.loop(0, 6)
    def _(i):
        @pl.when(i < 5)
        def _():
            j = 4 - i
            x = pair(0, j)
            PG[...] = nn(x, VG[...])
            ring_step(0, PG, j)
            PU[...] = nn(x, VU[...])
            ring_step(1, PU, j)

            @pl.when(j == 0)
            def _():
                low_wait()
                low = low_chunk(0)
                gate = ring_total(0, PG) + SCALE * nn(half_rows(low, True), BGU[...])
                up = ring_total(1, PU) + SCALE * nn(half_rows(low, False), BGU[...])
                GA[...] = gate
                UA[...] = up
                put_chunk(0, gate * jax.nn.sigmoid(gate) * up)
                chain_start(0, 1)

        @pl.when(i < 3)
        def _():
            near_step(0, 2 - i)
            near_step(1, 2 - i)

        @pl.when(i < 4)
        def _():
            near_step(2, 3 - i)

        @pl.when(i == 0)
        def _():
            spread_far(1)

        @pl.when(i == 1)
        def _():
            spread_wait(1, (3, 1, 2))

        @pl.when(i == 5)
        def _():
            chain_wait(0, 1)
            chain_start(0, 2)

        @pl.when(i > 0)
        def _():
            j = 5 - i
            PH[...] = nt(pair(1, j), VD[...])
            ring_step(2, PH, j)

            @pl.when(j == 0)
            def _():
                grad = ring_total(2, PH) + SCALE * nn(low_chunk(1)[:, 0:R], AD[...])
                gate, up = GA[...], UA[...]
                sigma = jax.nn.sigmoid(gate)
                put_chunk(1, grad * up * sigma * (1.0 + gate * (1.0 - sigma)))
                chain_start(1, 1)
                put_chunk(2, grad * gate * sigma)
                chain_start(2, 1)

        @pl.when(i == 1)
        def _():
            low_sum()

    def sib_copy(f, d):
        rows = pl.ds(pl.multiple_of((1 - c) * 32, 32), 32)
        return remote(ST.at[f, d, rows], SB.at[f, d], sbs.at[f, d], sbr.at[f, d], z, sibling)

    def sib_start(f, j):
        da, db = mod(z + NZ - j, NZ), mod(z + j, NZ)
        sib_copy(f, da).start()

        @pl.when((j > 0) & (j < 4))
        def _():
            sib_copy(f, db).start()

    def owner_copy(f, d, k):
        return remote(
            O2.at[f, d, pl.ds(k * TB, TB)], RX.at[f, q], rxs.at[f, 2 * d + k], rxr.at[f, q],
            z, owner(d, c, k),
        )

    def combine_one(f, d):
        sib_copy(f, d).wait_recv()
        rows = pl.ds(pl.multiple_of(c * 32, 32), 32)
        total = (ST[f, d, rows].astype(F32) + SB[f, d].astype(F32)).astype(BF16)
        O2[f, d] = total
        for k in range(2):
            own = owner(d, c, k) == g

            @pl.when(own)
            def _():
                RX[f, q] = total[k * TB : (k + 1) * TB]

            @pl.when(jnp.logical_not(own))
            def _():
                owner_copy(f, d, k).start()

    def combine(f, j):
        combine_one(f, mod(z + NZ - j, NZ))

        @pl.when((j > 0) & (j < 4))
        def _():
            combine_one(f, mod(z + j, NZ))

    def hpair(b, j):
        return jnp.concatenate([H[b, d].reshape(CH, FF) for d in (mod(z + NZ - j, NZ), mod(z + j, NZ))], axis=0)

    def adapter_grads(b, j, x):
        da, db = mod(z + NZ - j, NZ), mod(z + j, NZ)
        low = [LA[device_of(d, n), 0:TB] for d in (da, db) for n in (0, 2, 1, 3)]
        low = [jnp.where(mod(d, 2) == 0, low[4 * m + i], low[4 * m + (i + 2) % 4]) for m, d in enumerate((da, db)) for i in range(4)]
        low = jnp.concatenate(low, axis=0)
        once = (lax.broadcasted_iota(jnp.int32, (2 * CH, 128), 0) < CH) | (mod(j, 4) > 0)
        LOWF[b] += tn(jnp.where(once, low, jnp.zeros_like(low)), x)

    LOWF[...] = jnp.zeros((2, 128, FF), F32)

    def stage(f, j, wide, low, width):
        for n, d in enumerate((mod(z + NZ - j, NZ), mod(z + j, NZ))):
            ST[f, d, :, 0:D] = wide[n * CH : (n + 1) * CH].astype(BF16)
            ST[f, d, :, D : D + width] = low[n * CH : (n + 1) * CH].astype(BF16)

    ST[0, :, :, D + R : W] = jnp.zeros((NZ, CH, R), BF16)

    def rows_total(f):
        @pl.loop(0, NC)
        def _(s):
            @pl.when(s != q)
            def _():
                remote(RX.at[f, s], RX.at[f, s], rxs.at[f, 0], rxr.at[f, s], z, g).wait_recv()

        return jnp.sum(RX[f].astype(F32), axis=0)

    def chain_pass(b, j):
        @pl.when(j > 0)
        def _():
            chain_wait(b, j)

            @pl.when(j < 4)
            def _():
                chain_start(b, j + 1)

    @pl.loop(0, 6)
    def _(u):
        j = u - 1

        @pl.when((u > 1) & (u < 5))
        def _():
            chain_pass(0, u)

        @pl.when(u < 5)
        def _():
            x = hpair(0, u)
            stage(0, u, nn(x, VD[...]), nt(x, AD[...]), R)
            sib_start(0, u)

        @pl.when(j > 0)
        def _():
            combine(1, j - 1)

        @pl.when(j >= 0)
        def _():
            chain_pass(1, j)
            x = hpair(1, j)
            WIDE[:, 0:D] = nt(x, VG[...])
            WIDE[:, D:W] = nt(x, BGU[...])

        @pl.when(u < 5)
        def _():
            combine(0, u)

        @pl.when(u == 5)
        def _():
            total = rows_total(0)
            down_low = total[:, D : D + R].astype(BF16)
            DL[me, :, 0:R] = down_low

            @pl.loop(1, NG)
            def _(k):
                to_plane(DL, dls, dlr, k).start()

            out[...] = (total[:, 0:D] + SCALE * nn(down_low, BD[...])).astype(BF16)

        @pl.when(j >= 0)
        def _():
            chain_pass(2, j)
            x = hpair(2, j)
            lane = lax.broadcasted_iota(jnp.int32, (2 * CH, 128), 1)
            low = jnp.where(lane < R, WIDE[:, D:W], nt(x, BGU[...]))
            stage(1, j, WIDE[:, 0:D] + nt(x, VU[...]), low, 128)
            sib_start(1, j)
            adapter_grads(1, j, x)
            adapter_grads(0, j, hpair(1, j))

    for b, ref in ((0, gmap), (1, umap)):
        ref[...] = SCALE * LOWF[b, pl.ds(pl.multiple_of(R * b + 8 * z, 8), 8)]

    combine(1, 4)

    for a in range(2):
        for i in range(SIDE):
            for k in range(SIDE):
                if k:
                    far(a, me, i, k).wait_send()
                elif i:
                    near(a, me, i).wait_send()
                relay(a, me, i, k).wait_send()

    @pl.loop(1, NZ)
    def _(k):
        remote(LZ.at[z], LZ.at[z], lzs.at[k], lzr.at[k], z, g).wait_send()

    @pl.loop(1, NG)
    def _(k):
        to_plane(LA, las, lar, k).wait_send()

    for a in range(3):
        ring_copy(a, 0, 4, False).wait_send()
        for way in range(2):
            ring_copy(a, way, 4, True).wait_send()
            for j in range(1, 4):
                ring_copy(a, way, j, True).wait_send()
                ring_copy(a, way, j, False).wait_send()

    @pl.loop(1, NG)
    def _(k):
        from_plane(DL, dls, dlr, k).wait_recv()

    grads = SCALE * tn(DL[...].reshape(NG * TB, 128), X[1].reshape(NG * TB, D))
    rank = lax.broadcasted_iota(jnp.int32, (128, D), 0)
    for k in range(2):
        dmap[k : k + 1] = jnp.sum(jnp.where(rank == 2 * g + k, grads, 0.0), axis=0, keepdims=True)

    @pl.loop(1, NG)
    def _(k):
        to_plane(DL, dls, dlr, k).wait_send()

    for a in range(3):
        for way in range(2):
            chain_copy(a, way, 4, True, False).wait_send()
            for j in range(1, 4):
                chain_copy(a, way, j, False, False).wait_send()

    def owner_sent(f, d):
        for k in range(2):
            @pl.when(owner(d, c, k) != g)
            def _():
                owner_copy(f, d, k).wait_send()

    @pl.loop(0, NZ)
    def _(d):
        for f in range(2):
            sib_copy(f, d).wait_send()
        owner_sent(0, d)

        @pl.when(d != mod(z + 4, NZ))
        def _():
            owner_sent(1, d)

    total = rows_total(1)
    back = total[:, D:W].astype(BF16)
    tig[...] = (total[:, 0:D] + SCALE * nn(back, AGU[...])).astype(BF16)
    owner_sent(1, mod(z + 4, NZ))


def place(*refs):
    for a, b in zip(refs[:5], refs[5:]):
        b[...] = a[...]


def body(tok, wg, wu, wd, ag, au, ad, bg, bu, bd, cot):
    dma = pltpu.SemaphoreType.DMA
    hbm = pl.BlockSpec(memory_space=pltpu.HBM)
    vmem = pl.BlockSpec(memory_space=pltpu.VMEM)
    args = (tok, wg, wu, wd, ag.T, au.T, ad.T, bg, bu, bd, cot)
    results = pl.pallas_call(
        kernel,
        out_shape=(
            jax.ShapeDtypeStruct((TB, D), BF16),
            jax.ShapeDtypeStruct((TB, D), BF16),
            jax.ShapeDtypeStruct((8, FF), F32),
            jax.ShapeDtypeStruct((8, FF), F32),
            jax.ShapeDtypeStruct((2, D), F32),
        ),
        in_specs=[hbm] * 11,
        out_specs=(vmem,) * 5,
        scratch_shapes=[
            pltpu.VMEM((2, NG, TB, D), BF16),
            pltpu.VMEM((D, FF), BF16),
            pltpu.VMEM((D, FF), BF16),
            pltpu.VMEM((FF, D), BF16),
            pltpu.VMEM((2 * R, D), BF16),
            pltpu.VMEM((R, FF), BF16),
            pltpu.VMEM((2 * R, FF), BF16),
            pltpu.VMEM((R, D), BF16),
            pltpu.VMEM((NZ, 2 * TB, 128), BF16),
            pltpu.VMEM((NG, 2 * TB, 128), BF16),
            pltpu.VMEM((NG, TB, 128), BF16),
            pltpu.VMEM((3, NZ, TB, FF), F32),
            pltpu.VMEM((6 * TB, FF), F32),
            pltpu.VMEM((6 * TB, FF), F32),
            pltpu.VMEM((6 * TB, FF), F32),
            pltpu.VMEM((2 * CH, W), F32),
            pltpu.VMEM((CH, FF), F32),
            pltpu.VMEM((CH, FF), F32),
            pltpu.VMEM((3, 2, 4, 4, TB, FF), BF16),
            pltpu.VMEM((3, 2, 5, 4, TB, FF), BF16),
            pltpu.VMEM((3, NZ, 4, TB, FF), BF16),
            pltpu.VMEM((2, NZ, CH, W), BF16),
            pltpu.VMEM((2, NZ, CH // 2, W), BF16),
            pltpu.VMEM((2, NZ, CH // 2, W), BF16),
            pltpu.VMEM((2, NC, TB, W), BF16),
            pltpu.VMEM((2, 128, FF), F32),
            dma((9,)),
            dma((2,)),
            dma((2, SIDE)),
            dma((2, SIDE)),
            dma((2, SIDE, SIDE)),
            dma((2, SIDE, SIDE)),
            dma((2, SIDE, SIDE)),
            dma((2, SIDE, SIDE)),
            dma((NZ,)),
            dma((NZ,)),
            dma((NG,)),
            dma((NG,)),
            dma((NG,)),
            dma((NG,)),
            dma((3, 2, 8)),
            dma((3, 2, 8)),
            dma((3, 2, 4)),
            dma((3, 2, 4)),
            dma((2, NZ)),
            dma((2, NZ)),
            dma((2, 2 * NZ)),
            dma((2, NC)),
        ],
        compiler_params=pltpu.CompilerParams(
            collective_id=0, has_side_effects=True, vmem_limit_bytes=VMEM
        ),
    )(*args)
    return pl.pallas_call(
        place,
        out_shape=tuple(jax.ShapeDtypeStruct(r.shape, r.dtype) for r in results),
        in_specs=[vmem] * 5,
        out_specs=(vmem,) * 5,
    )(*results)


def solution(mesh):
    in_specs = (
        P("gy", "gx"),
        P("gx", "gy"),
        P("gx", "gy"),
        P("gy", "gx"),
        P("gx", None),
        P("gx", None),
        P("gy", None),
        P(None, "gy"),
        P(None, "gy"),
        P(None, "gx"),
        P("gy", "gx"),
    )
    out_specs = (P("gy", "gx"), P("gy", "gx"), P("gx", "gy"), P("gx", "gy"), P("gy", "gx"))
    return jax.shard_map(body, mesh=mesh, in_specs=in_specs, out_specs=out_specs, check_vma=False)
```
